32 devices in a mesh: tm: 16 (over z, x, core), band: 2 (over y).
Axes of the slice: x: 2, y: 2, z: 4, core: 2. Of those that a mesh axis runs over, the one named last changes fastest.
Arguments:
- query_input: bfloat16 [16, 10, 26, 1120], P('tm', 'band'), may hold values from -6 to 6
- key_input: bfloat16 [16, 10, 26, 1120], P('tm', 'band'), may hold values from -8 to 8
- value_input: bfloat16 [16, 10, 26, 1120], P('tm', 'band'), may hold values from -12 to 12
- cotangent: bfloat16 [16, 10, 26, 1120], P('tm', 'band'), may hold values from -6 to 6
- local_kernel_weight: float32 [3, 3, 1120], replicated, may hold values from -2 to 2
Outputs:
- mixed_out: bfloat16 [16, 10, 26, 1120], P('tm', 'band')
- query_grad: bfloat16 [16, 10, 26, 1120], P('tm', 'band')
- key_grad: bfloat16 [16, 10, 26, 1120], P('tm', 'band')
- value_grad: bfloat16 [16, 10, 26, 1120], P('tm', 'band')
- kernel_grad: float32 [3, 3, 1120], replicated
The draws below stay inside these ranges and needn't reach their ends.
All inputs are finite; a program needn't handle non-finite values.
Results may differ from the reference program's by a relative error of at most 0.018.
Values may be sent and summed in bfloat16 or wider, within the bound.
A program may use at most 128 MiB of HBM per device.

```python
import jax
import jax.numpy as jnp
from jax import lax

HEADS = 35
HEAD_DIM = 32
D = 1120
FRAME_COLUMNS = 26
FRAMES = 16
FRAME_ROWS = 10
TOKENS = 4160


def token_shape():
    return (FRAMES, FRAME_ROWS, FRAME_COLUMNS, D)


def noise_field(key, shape):
    return jax.random.normal(key, shape, jnp.float32)


def head_factor(key, salt):
    factor = noise_field(jax.random.fold_in(key, salt), (FRAMES, FRAME_ROWS, FRAME_COLUMNS, HEADS, 1))
    return jnp.broadcast_to(factor, (FRAMES, FRAME_ROWS, FRAME_COLUMNS, HEADS, HEAD_DIM)).reshape(token_shape())


def channel_weight(key, salt, lower, upper):
    magnitude = jax.random.uniform(jax.random.fold_in(key, salt), (D,), jnp.float32, lower, upper)
    flipper = jax.random.uniform(jax.random.fold_in(key, salt + 1), (D,), jnp.float32)
    return jnp.where(flipper < 0.5, -magnitude, magnitude)


def frame_offset(key, salt, normal_scale):
    shape = (FRAMES, 1, 1, D)
    return normal_scale * jax.random.normal(jax.random.fold_in(key, salt), shape, jnp.float32)


def draw_key_input(key, part):
    shared = head_factor(key, 5)
    own_noise = noise_field(jax.random.fold_in(key, 11), token_shape())
    offset = frame_offset(key, 12, 1.2)
    return jnp.clip(0.8 * shared + 0.6 * own_noise + offset, -8.0, 8.0).astype(jnp.bfloat16)


def draw_value_input(key, part):
    shared = head_factor(key, 5)
    key_noise = noise_field(jax.random.fold_in(key, 11), token_shape())
    coupling = channel_weight(key, 31, 1.2, 1.8)
    own_noise = noise_field(jax.random.fold_in(key, 23), token_shape())
    offset = frame_offset(key, 24, 2.5)
    total = coupling * shared + 0.8 * key_noise + 0.6 * own_noise + offset
    return jnp.clip(total, -12.0, 12.0).astype(jnp.bfloat16)


def draw_query_input(key, part):
    shared = head_factor(key, 41)
    own_noise = noise_field(jax.random.fold_in(key, 43), token_shape())
    return jnp.clip(1.5 * (0.6 * shared + 0.8 * own_noise), -6.0, 6.0).astype(jnp.bfloat16)


def draw_cotangent(key, part):
    shared = head_factor(key, 41)
    query_noise = noise_field(jax.random.fold_in(key, 43), token_shape())
    coupling = channel_weight(key, 47, 0.6, 1.0)
    own_noise = noise_field(jax.random.fold_in(key, 53), token_shape())
    total = coupling * shared + 0.5 * query_noise + 0.6 * own_noise
    return jnp.clip(total, -6.0, 6.0).astype(jnp.bfloat16)


def centred(stream_key, extent, deviation, bound, held_as=jnp.bfloat16):
    result = deviation * jax.random.normal(stream_key, extent, jnp.float32)
    return jnp.clip(result, min=-bound, max=bound).astype(held_as)


def setup_inputs(seed: int = 0) -> dict:
    seeds = jax.random.split(jax.random.key(seed), 6)
    query_input = draw_query_input(jax.random.fold_in(seeds[5], 71), 0)
    key_input = draw_key_input(jax.random.fold_in(seeds[5], 71), 0)
    value_input = draw_value_input(jax.random.fold_in(seeds[5], 71), 0)
    cotangent = draw_cotangent(jax.random.fold_in(seeds[5], 71), 0)
    local_kernel_weight = centred(seeds[4], (3, 3, D), 9 ** -0.5, 2.0, jnp.float32)
    return {"query_input": query_input, "key_input": key_input, "value_input": value_input, "cotangent": cotangent, "local_kernel_weight": local_kernel_weight}


def feature(x):
    return jnp.where(x > 0, x + 1.0, jnp.exp(jnp.minimum(x, 0.0)))

def slope(x):
    return jnp.where(x > 0, jnp.ones_like(x), jnp.exp(jnp.minimum(x, 0.0)))

def heads_of(x):
    return x.reshape(FRAME_ROWS * FRAME_COLUMNS, HEADS, HEAD_DIM)

def padded_frame_helper(x):
    return jnp.pad(x, ((1, 1), (1, 1), (0, 0)))

def reference(query_input, key_input, value_input, cotangent, local_kernel_weight):
    high = lax.Precision.HIGHEST

    def frame_terms(items):
        query, keyed, value_tensor = items
        key_feat = feature(heads_of(keyed).astype(jnp.float32)).astype(jnp.bfloat16)
        state = jnp.einsum('thd,the->hde', key_feat.astype(jnp.float32), heads_of(value_tensor).astype(jnp.float32), precision=high)
        norm_vec = lax.optimization_barrier(jnp.sum(key_feat.astype(jnp.float32), axis=0))
        return (state, norm_vec)
    frame_state, frame_norm = lax.map(frame_terms, (query_input, key_input, value_input))
    state_all = jnp.cumsum(frame_state, axis=0)
    norm_all = jnp.cumsum(frame_norm, axis=0)

    def frame_forward(items):
        query, value_tensor, grad, state, norm_vec = items
        q_raw = heads_of(query).astype(jnp.float32)
        q_feat = feature(q_raw).astype(jnp.bfloat16).astype(jnp.float32)
        num = jnp.einsum('thd,hde->the', q_feat, state, precision=high)
        den = jnp.einsum('thd,hd->th', q_feat, norm_vec, precision=high)
        attn = num / den[:, :, None]
        value_padded = padded_frame_helper(value_tensor).astype(jnp.float32)
        gpad = padded_frame_helper(grad).astype(jnp.float32)
        local_output = jnp.zeros((FRAME_ROWS, FRAME_COLUMNS, D), jnp.float32)
        v_local = jnp.zeros((FRAME_ROWS, FRAME_COLUMNS, D), jnp.float32)
        gradient_whole = grad.astype(jnp.float32)
        kernel_row_slice = []
        for row_offset in range(3):
            for column_offset in range(3):
                local_output = local_output + local_kernel_weight[row_offset, column_offset] * value_padded[row_offset:row_offset + FRAME_ROWS, column_offset:column_offset + FRAME_COLUMNS]
                v_local = v_local + local_kernel_weight[row_offset, column_offset] * gpad[2 - row_offset:2 - row_offset + FRAME_ROWS, 2 - column_offset:2 - column_offset + FRAME_COLUMNS]
                kernel_row_slice.append(lax.optimization_barrier(jnp.sum(gradient_whole * value_padded[row_offset:row_offset + FRAME_ROWS, column_offset:column_offset + FRAME_COLUMNS], axis=(0, 1))))
        mixed = (attn.reshape(FRAME_ROWS, FRAME_COLUMNS, D) + local_output).astype(jnp.bfloat16)
        g_heads = heads_of(gradient_whole)
        scaled = g_heads / den[:, :, None]
        den_grad = -lax.optimization_barrier(jnp.sum(g_heads * attn, axis=2)) / den
        back_state = jnp.einsum('thd,the->hde', q_feat, scaled, precision=high)
        back_norm = jnp.einsum('thd,th->hd', q_feat, den_grad, precision=high)
        q_grad = jnp.einsum('the,hde->thd', scaled, state, precision=high) + den_grad[:, :, None] * norm_vec[None]
        q_grad = (q_grad * slope(q_raw)).reshape(FRAME_ROWS, FRAME_COLUMNS, D).astype(jnp.bfloat16)
        return (mixed, q_grad, back_state, back_norm, v_local, jnp.stack(kernel_row_slice).reshape(3, 3, D))
    mixed_out, query_grad, back_state, back_norm, v_local, kernel_terms = lax.map(frame_forward, (query_input, value_input, cotangent, state_all, norm_all))
    later_state = jnp.flip(jnp.cumsum(jnp.flip(back_state, 0), axis=0), 0)
    later_norm = jnp.flip(jnp.cumsum(jnp.flip(back_norm, 0), axis=0), 0)

    def frame_backward(items):
        keyed, value_tensor, local_part, state, norm_vec = items
        k_raw = heads_of(keyed).astype(jnp.float32)
        key_feat = feature(k_raw).astype(jnp.bfloat16).astype(jnp.float32)
        k_grad = jnp.einsum('the,hde->thd', heads_of(value_tensor).astype(jnp.float32), state, precision=high) + norm_vec[None]
        k_grad = (k_grad * slope(k_raw)).reshape(FRAME_ROWS, FRAME_COLUMNS, D).astype(jnp.bfloat16)
        v_grad = jnp.einsum('thd,hde->the', key_feat, state, precision=high).reshape(FRAME_ROWS, FRAME_COLUMNS, D) + local_part
        return (k_grad, v_grad.astype(jnp.bfloat16))
    key_grad, value_grad = lax.map(frame_backward, (key_input, value_input, v_local, later_state, later_norm))
    kernel_grad = lax.optimization_barrier(jnp.sum(kernel_terms, axis=0)) / jnp.sqrt(jnp.float32(TOKENS))
    return (mixed_out, query_grad, key_grad, value_grad, kernel_grad)
```

```python
import functools
import math

import jax
import jax.numpy as jnp
from jax import lax
from jax.experimental import pallas as pl
from jax.experimental.pallas import tpu as pltpu
from jax.sharding import PartitionSpec as P

HEAD_DIM = 32
LANES = 128
COLS = 32
MESH = pl.DeviceIdType.MESH
F32 = jnp.float32
BF16 = jnp.bfloat16


def groups(wide):
    out, at = [], 0
    while at < wide:
        size = min(256, wide - at)
        out.append((at, size))
        at += size
    return out


def feature(x):
    return jnp.where(x > 0, x + 1.0, jnp.exp(jnp.minimum(x, 0.0)))


def slope(x):
    return jnp.where(x > 0, 1.0, jnp.exp(jnp.minimum(x, 0.0)))


def parts_of(x):
    high = x.astype(BF16)
    return high, (x - high.astype(F32)).astype(BF16)


def mm(a, b):
    return lax.dot_general(a, b, (((1,), (0,)), ((), ())), preferred_element_type=F32)


def mm_bt(a, b):
    return lax.dot_general(a, b, (((1,), (1,)), ((), ())), preferred_element_type=F32)


def mm_at(a, b):
    return lax.dot_general(a, b, (((0,), (0,)), ((), ())), preferred_element_type=F32)


def same_head(size):
    row = lax.broadcasted_iota(jnp.int32, (size, size), 0) // HEAD_DIM
    lane = lax.broadcasted_iota(jnp.int32, (size, size), 1) // HEAD_DIM
    return row == lane


def compress(full, mask):
    size = full.shape[0]
    kept = jnp.where(mask, full, 0.0)
    total = kept[0:HEAD_DIM]
    for h in range(1, size // HEAD_DIM):
        total = total + kept[h * HEAD_DIM : (h + 1) * HEAD_DIM]
    return total


def expand(compact, mask):
    size = compact.shape[1]
    tiled = jnp.concatenate([compact] * (size // HEAD_DIM), axis=0)
    return parts_of(jnp.where(mask, tiled, 0.0))


def kernel(cfg, q_hbm, k_hbm, v_hbm, g_hbm, w_ref, mixed_ref, qg_ref, kg_ref, vg_ref, wg_ref,
           q_raw, k_raw, v_raw, g_raw, halo, vpad, gpad, qf, kf, wpad, loc, vloc, kterm,
           attn_s, rden_s, dgw_s, state, src_f, r1_f, tot_f, r2_f, res_f, r3_f,
           src_b, r1_b, tot_b, r2_b, res_b, r3_b,
           in_sem, halo_send, halo_recv, s1, v1, s2, v2, s3, v3):
    rows, cols, width, wide, nb, no, inner, kr = cfg
    group = nb * inner
    share = HEAD_DIM // group
    count = rows * COLS
    tm = lax.axis_index("tm")
    band = lax.axis_index("band")
    z = tm // inner
    a = tm % inner
    m = a * nb + band

    def peer_of(o):
        p = (m + o) % group
        return p, {"tm": z * inner + p // nb, "band": p % nb}

    def outer_of(o):
        zp = (z + o) % no
        return zp, {"tm": zp * inner + a, "band": band}

    loads = [
        pltpu.make_async_copy(h.at[0], d, in_sem.at[i])
        for i, (h, d) in enumerate(((k_hbm, k_raw), (v_hbm, v_raw), (q_hbm, q_raw), (g_hbm, g_raw)))
    ]
    for c in loads:
        c.start()
    halo[...] = jnp.zeros_like(halo)
    barrier = pltpu.get_barrier_semaphore()
    for o in range(1, group):
        pl.semaphore_signal(barrier, inc=1, device_id=peer_of(o)[1], device_id_type=MESH)
    for o in range(1, no):
        pl.semaphore_signal(barrier, inc=1, device_id=outer_of(o)[1], device_id_type=MESH)

    vpad[...] = jnp.zeros_like(vpad)
    gpad[...] = jnp.zeros_like(gpad)
    kf[...] = jnp.zeros_like(kf)
    kf[:, 0:cols, width:wide] = jnp.ones((rows, cols, wide - width), BF16)
    qf[...] = jnp.ones_like(qf)
    wpad[...] = jnp.zeros_like(wpad)
    for i in range(3):
        for j in range(3):
            wpad[3 * i + j : 3 * i + j + 1, 0:width] = w_ref[i, j : j + 1, :]
    src_f[...] = jnp.zeros_like(src_f)
    src_b[...] = jnp.zeros_like(src_b)

    pl.semaphore_wait(barrier, group - 1 + no - 1)

    def halo_copies(up):
        out = []
        for i, h in enumerate((v_hbm, g_hbm)):
            out.append(pltpu.make_async_remote_copy(
                src_ref=h.at[0, 0] if up else h.at[0, rows - 1],
                dst_ref=halo.at[i, 1 if up else 0],
                send_sem=halo_send.at[i, 1 if up else 0],
                recv_sem=halo_recv.at[i, 1 if up else 0],
                device_id={"band": band - 1 if up else band + 1},
                device_id_type=MESH,
            ))
        return out

    @pl.when(band > 0)
    def _():
        for c in halo_copies(True):
            c.start()

    @pl.when(band < nb - 1)
    def _():
        for c in halo_copies(False):
            c.start()

    masks = {size: same_head(size) for _, size in groups(wide)}
    ones = {size: masks[size].astype(F32).astype(BF16) for size in masks}

    def put(src, at, size, compact, norm):
        for j in range(group):
            src[j, 0:share, at : at + size] = compact[share * j : share * (j + 1)]
            src[j, share : share + 1, at : at + size] = norm

    def phase1(way, src, r1):
        out = []
        for o in range(1, group):
            p, dev = peer_of(o)
            c = pltpu.make_async_remote_copy(
                src_ref=src.at[p], dst_ref=r1.at[m], send_sem=s1.at[way, o],
                recv_sem=v1.at[way, m], device_id=dev, device_id_type=MESH)
            c.start()
            out.append(c)
        r1[pl.ds(m, 1)] = src[pl.ds(m, 1)]
        return out

    def wait1(way, src, r1):
        for o in range(1, group):
            p, dev = peer_of(o)
            pltpu.make_async_remote_copy(
                src_ref=src.at[p], dst_ref=r1.at[p], send_sem=s1.at[way, o],
                recv_sem=v1.at[way, p], device_id=dev, device_id_type=MESH).wait_recv()

    def phase2(way, r1, tot, r2):
        total = r1[0]
        for j in range(1, group):
            total = total + r1[j]
        tot[...] = total
        out = []
        for o in range(1, no):
            zp, dev = outer_of(o)
            c = pltpu.make_async_remote_copy(
                src_ref=tot, dst_ref=r2.at[z], send_sem=s2.at[way, o],
                recv_sem=v2.at[way, z], device_id=dev, device_id_type=MESH)
            c.start()
            out.append(c)
        r2[pl.ds(z, 1)] = total[None]
        return out

    def wait2(way, tot, r2):
        for o in range(1, no):
            zp, dev = outer_of(o)
            pltpu.make_async_remote_copy(
                src_ref=tot, dst_ref=r2.at[zp], send_sem=s2.at[way, o],
                recv_sem=v2.at[way, zp], device_id=dev, device_id_type=MESH).wait_recv()

    def phase3(way, r1, r2, res, r3):
        backward = way == 1
        run = jnp.zeros_like(r2[0])
        whole = run
        for zz in range(no):
            part = r2[zz]
            earlier = (zz > z) if backward else (zz < z)
            run = run + jnp.where(earlier, part, 0.0)
            whole = whole + part
        extra = lax.broadcasted_iota(jnp.int32, run.shape, 0) > share
        for aa in (range(inner - 1, -1, -1) if backward else range(inner)):
            for bb in range(nb):
                run = run + r1[aa * nb + bb]
            res[aa] = jnp.where(extra, whole, run) if backward else run
        out = []
        for o in range(1, group):
            p, dev = peer_of(o)
            c = pltpu.make_async_remote_copy(
                src_ref=res.at[p // nb], dst_ref=r3.at[m], send_sem=s3.at[way, o],
                recv_sem=v3.at[way, m], device_id=dev, device_id_type=MESH)
            c.start()
            out.append(c)
        r3[pl.ds(m, 1)] = res[pl.ds(a, 1)]
        return out

    def wait3(way, res, r3):
        for o in range(1, group):
            p, dev = peer_of(o)
            pltpu.make_async_remote_copy(
                src_ref=res.at[p // nb], dst_ref=r3.at[p], send_sem=s3.at[way, o],
                recv_sem=v3.at[way, p], device_id=dev, device_id_type=MESH).wait_recv()
        for j in range(group):
            state[share * j : share * (j + 1), :] = r3[j, 0:share, :]

    sent = []
    loads[0].wait()
    kf[:, 0:cols, 0:width] = feature(k_raw[...].astype(F32)).astype(BF16)
    loads[1].wait()
    vpad[1 : rows + 1, 0:cols, 0:width] = v_raw[...].astype(F32)
    for at, size in groups(wide):
        kg = kf[:, :, at : at + size].reshape(count, size)
        vg = vpad[1 : rows + 1, :, at : at + size].reshape(count, size).astype(BF16)
        own = compress(mm_at(kg, vg), masks[size])
        norm = jnp.sum(kg.astype(F32), axis=0, keepdims=True)
        put(src_f, at, size, own, norm)
    sent += phase1(0, src_f, r1_f)
    loads[2].wait()
    qf[:, 0:cols, 0:width] = feature(q_raw[...].astype(F32)).astype(BF16)
    loads[3].wait()
    gpad[1 : rows + 1, 0:cols, 0:width] = g_raw[...].astype(F32)

    def conv(t):
        lanes = pl.ds(pl.multiple_of(t * LANES, LANES), LANES)
        vb = vpad[:, :, lanes]
        gb = gpad[:, :, lanes]
        vs = (pltpu.roll(vb, 1, 1), vb, pltpu.roll(vb, COLS - 1, 1))
        gs = (pltpu.roll(gb, 1, 1), gb, pltpu.roll(gb, COLS - 1, 1))
        own = gb[1 : rows + 1]
        lo = jnp.zeros((rows, COLS, LANES), F32)
        vl = lo
        for i in range(3):
            for j in range(3):
                w = wpad[3 * i + j : 3 * i + j + 1, lanes].reshape(1, 1, LANES)
                near = vs[j][i : i + rows]
                lo = lo + w * near
                vl = vl + w * gs[2 - j][2 - i : 2 - i + rows]
                term = jnp.sum(jnp.sum(own * near, axis=0), axis=0, keepdims=True)
                kterm[3 * i + j : 3 * i + j + 1, lanes] = term
        loc[:, :, lanes] = lo
        vloc[:, :, lanes] = vl

    tiles = wide // LANES
    half = (tiles + 1) // 2
    wait1(0, src_f, r1_f)
    sent += phase2(0, r1_f, tot_f, r2_f)

    @pl.when(band > 0)
    def _():
        for c in halo_copies(False):
            c.wait_recv()

    @pl.when(band < nb - 1)
    def _():
        for c in halo_copies(True):
            c.wait_recv()

    for i, pad in enumerate((vpad, gpad)):
        pad[0, 0:cols, 0:width] = halo[i, 0].astype(F32)
        pad[rows + 1, 0:cols, 0:width] = halo[i, 1].astype(F32)
    pl.loop(0, half)(conv)
    wait2(0, tot_f, r2_f)
    sent += phase3(0, r1_f, r2_f, res_f, r3_f)
    pl.loop(half, tiles)(conv)
    for r in range(9):
        src_b[r // kr, share + 1 + r % kr : share + 2 + r % kr, :] = kterm[r : r + 1, :]
    wait3(0, res_f, r3_f)
    blocks = []
    for at, size in groups(wide):
        mask, one = masks[size], ones[size]
        high, low = expand(state[:, at : at + size], mask)
        norm = r3_f[0, share : share + 1, at : at + size]
        blocks.append((high, low, norm))
        qg = qf[:, :, at : at + size].reshape(count, size)
        gg = gpad[1 : rows + 1, :, at : at + size].reshape(count, size)
        dh, dl = parts_of(qg.astype(F32) * norm)
        den = mm(dh, one) + mm(dl, one)
        num = mm(qg, high) + mm(qg, low)
        rden = 1.0 / den
        attn = num * rden
        th, tl = parts_of(gg * attn)
        dgw = -(mm(th, one) + mm(tl, one)) * rden
        sh, sl = parts_of(gg * rden)
        own = compress(mm_at(qg, sh) + mm_at(qg, sl), mask)
        put(src_b, at, size, own, jnp.sum(qg.astype(F32) * dgw, axis=0, keepdims=True))
        attn_s[:, at : at + size] = attn
        rden_s[:, at : at + size] = rden
        dgw_s[:, at : at + size] = dgw
    sent += phase1(1, src_b, r1_b)
    mixed = (attn_s[...].reshape(rows, COLS, wide) + loc[...]).astype(BF16)
    mixed_ref[0] = mixed[:, 0:cols, 0:width]
    wait1(1, src_b, r1_b)
    sent += phase2(1, r1_b, tot_b, r2_b)
    for (at, size), (high, low, norm) in zip(groups(wide), blocks):
        gg = gpad[1 : rows + 1, :, at : at + size].reshape(count, size)
        sh, sl = parts_of(gg * rden_s[:, at : at + size])
        back = mm_bt(sh, high) + mm_bt(sh, low) + mm_bt(sl, high)
        attn_s[:, at : at + size] = back + dgw_s[:, at : at + size] * norm
    grad = attn_s[...].reshape(rows, COLS, wide)[:, 0:cols, 0:width]
    qg_ref[0] = (grad * slope(q_raw[...].astype(F32))).astype(BF16)
    wait2(1, tot_b, r2_b)
    sent += phase3(1, r1_b, r2_b, res_b, r3_b)
    wait3(1, res_b, r3_b)
    for at, size in groups(wide):
        high, low = expand(state[:, at : at + size], masks[size])
        norm = r3_b[0, share : share + 1, at : at + size]
        kg = kf[:, :, at : at + size].reshape(count, size)
        vg = vpad[1 : rows + 1, :, at : at + size].reshape(count, size).astype(BF16)
        attn_s[:, at : at + size] = mm_bt(vg, high) + mm_bt(vg, low) + norm
        rden_s[:, at : at + size] = mm(kg, high) + mm(kg, low)
    grad = attn_s[...].reshape(rows, COLS, wide)[:, 0:cols, 0:width]
    kg_ref[0] = (grad * slope(k_raw[...].astype(F32))).astype(BF16)
    vgrad = (rden_s[...].reshape(rows, COLS, wide) + vloc[...]).astype(BF16)
    vg_ref[0] = vgrad[:, 0:cols, 0:width]
    tokens = lax.axis_size("tm") * nb * rows * cols
    for r in range(9):
        line = r3_b[r // kr, share + 1 + r % kr : share + 2 + r % kr, 0:width]
        wg_ref[r // 3, r % 3 : r % 3 + 1, :] = line * (1.0 / math.sqrt(tokens))

    for c in sent:
        c.wait_send()

    @pl.when(band > 0)
    def _():
        for c in halo_copies(True):
            c.wait_send()

    @pl.when(band < nb - 1)
    def _():
        for c in halo_copies(False):
            c.wait_send()


def shards(query_input, key_input, value_input, cotangent, local_kernel_weight):
    _, rows, cols, width = query_input.shape
    wide = -(-width // LANES) * LANES
    frames, nb = lax.axis_size("tm"), lax.axis_size("band")
    inner = 4
    no = frames // inner
    group = nb * inner
    share = HEAD_DIM // group
    kr = -(-9 // group)
    rf, rb = share + 1, share + 1 + kr
    count = rows * COLS
    cfg = (rows, cols, width, wide, nb, no, inner, kr)
    raw = pltpu.VMEM((rows, cols, width), BF16)

    def buffers(r):
        return [
            pltpu.VMEM((group, r, wide), F32), pltpu.VMEM((group, r, wide), F32),
            pltpu.VMEM((r, wide), F32), pltpu.VMEM((no, r, wide), F32),
            pltpu.VMEM((inner, r, wide), F32), pltpu.VMEM((group, r, wide), F32),
        ]

    tok = jax.ShapeDtypeStruct(query_input.shape, BF16)
    dma = pltpu.SemaphoreType.DMA
    vm = pl.BlockSpec(memory_space=pltpu.VMEM)
    return pl.pallas_call(
        functools.partial(kernel, cfg),
        out_shape=(tok, tok, tok, tok, jax.ShapeDtypeStruct(local_kernel_weight.shape, F32)),
        in_specs=[pl.BlockSpec(memory_space=pl.ANY)] * 4 + [vm],
        out_specs=[vm] * 5,
        scratch_shapes=[
            raw, raw, raw, raw,
            pltpu.VMEM((2, 2, cols, width), BF16),
            pltpu.VMEM((rows + 2, COLS, wide), F32), pltpu.VMEM((rows + 2, COLS, wide), F32),
            pltpu.VMEM((rows, COLS, wide), BF16), pltpu.VMEM((rows, COLS, wide), BF16),
            pltpu.VMEM((16, wide), F32),
            pltpu.VMEM((rows, COLS, wide), F32), pltpu.VMEM((rows, COLS, wide), F32),
            pltpu.VMEM((16, wide), F32),
            pltpu.VMEM((count, wide), F32), pltpu.VMEM((count, wide), F32),
            pltpu.VMEM((count, wide), F32),
            pltpu.VMEM((HEAD_DIM, wide), F32),
            *buffers(rf), *buffers(rb),
            dma((4,)), dma((2, 2)), dma((2, 2)),
            dma((2, group)), dma((2, group)), dma((2, no)), dma((2, no)),
            dma((2, group)), dma((2, group)),
        ],
        compiler_params=pltpu.CompilerParams(
            collective_id=0, has_side_effects=True, vmem_limit_bytes=40 * 1024 * 1024
        ),
        cost_estimate=pl.CostEstimate(flops=10**9, bytes_accessed=3 * 10**6, transcendentals=0),
        name="block_causal",
    )(query_input, key_input, value_input, cotangent, local_kernel_weight)


def solution(mesh):
    token = P("tm", "band", None, None)
    return jax.shard_map(
        shards,
        mesh=mesh,
        in_specs=(token,) * 4 + (P(),),
        out_specs=(token,) * 4 + (P(),),
        check_vma=False,
    )
```

```python
import functools
import math

import jax
import jax.numpy as jnp
from jax import lax
from jax.experimental import pallas as pl
from jax.experimental.pallas import tpu as pltpu
from jax.sharding import PartitionSpec as P

HEAD_DIM = 32
LANES = 128
COLS = 32
MESH = pl.DeviceIdType.MESH
F32 = jnp.float32
BF16 = jnp.bfloat16


def groups(wide):
    out, at = [], 0
    while at < wide:
        size = min(256, wide - at)
        out.append((at, size))
        at += size
    return out


def feature(x):
    return jnp.where(x > 0, x + 1.0, jnp.exp(jnp.minimum(x, 0.0)))


def slope(x):
    return jnp.where(x > 0, 1.0, jnp.exp(jnp.minimum(x, 0.0)))


def parts_of(x):
    high = x.astype(BF16)
    return high, (x - high.astype(F32)).astype(BF16)


def mm(a, b):
    return lax.dot_general(a, b, (((1,), (0,)), ((), ())), preferred_element_type=F32)


def mm_bt(a, b):
    return lax.dot_general(a, b, (((1,), (1,)), ((), ())), preferred_element_type=F32)


def mm_at(a, b):
    return lax.dot_general(a, b, (((0,), (0,)), ((), ())), preferred_element_type=F32)


def same_head(size):
    row = lax.broadcasted_iota(jnp.int32, (size, size), 0) // HEAD_DIM
    lane = lax.broadcasted_iota(jnp.int32, (size, size), 1) // HEAD_DIM
    return row == lane


def compress(full, mask):
    size = full.shape[0]
    kept = jnp.where(mask, full, 0.0)
    total = kept[0:HEAD_DIM]
    for h in range(1, size // HEAD_DIM):
        total = total + kept[h * HEAD_DIM : (h + 1) * HEAD_DIM]
    return total


def expand(compact, mask):
    size = compact.shape[1]
    tiled = jnp.concatenate([compact] * (size // HEAD_DIM), axis=0)
    return parts_of(jnp.where(mask, tiled, 0.0))


def kernel(cfg, q_hbm, k_hbm, v_hbm, g_hbm, w_hbm, mixed_ref, qg_ref, kg_ref, vg_ref, wg_ref,
           q_raw, k_raw, v_raw, g_raw, halo, vpad, gpad, qf, kf, wpad, loc, vloc, kterm,
           attn_s, rden_s, dgw_s, state, stage, extra_s, w_raw, src_f, r1_f, tot_f, r2_f, res_f, r3_f,
           src_b, r1_b, tot_b, r2_b, res_b, r3_b,
           in_sem, halo_send, halo_recv, s1, v1, s2, v2, s3, v3):
    rows, cols, width, wide, nb, no, inner, per, first = cfg
    group = nb * inner
    share = HEAD_DIM // group
    count = rows * COLS
    tm = lax.axis_index("tm")
    band = lax.axis_index("band")
    z = tm // inner
    tiles = wide // LANES
    a = tm % inner
    m = a * nb + band

    def peer_of(o):
        p = (m + o) % group
        return p, {"tm": z * inner + p // nb, "band": p % nb}

    def outer_of(o):
        zp = (z + o) % no
        return zp, {"tm": zp * inner + a, "band": band}

    loads = [
        pltpu.make_async_copy(h.at[0], d, in_sem.at[i])
        for i, (h, d) in enumerate(((k_hbm, k_raw), (v_hbm, v_raw), (q_hbm, q_raw), (g_hbm, g_raw)))
    ]
    loads.append(pltpu.make_async_copy(w_hbm, w_raw, in_sem.at[4]))
    for c in loads:
        c.start()
    halo[...] = jnp.zeros_like(halo)
    barrier = pltpu.get_barrier_semaphore()
    for o in range(1, group):
        pl.semaphore_signal(barrier, inc=1, device_id=peer_of(o)[1], device_id_type=MESH)
    for o in range(1, no):
        pl.semaphore_signal(barrier, inc=1, device_id=outer_of(o)[1], device_id_type=MESH)

    vpad[...] = jnp.zeros_like(vpad)
    gpad[...] = jnp.zeros_like(gpad)
    kf[...] = jnp.zeros_like(kf)
    kf[:, 0:cols, width:wide] = jnp.ones((rows, cols, wide - width), BF16)
    qf[...] = jnp.ones_like(qf)
    wpad[...] = jnp.zeros_like(wpad)
    src_f[...] = jnp.zeros_like(src_f)
    stage[...] = jnp.zeros_like(stage)

    pl.semaphore_wait(barrier, group - 1 + no - 1)

    def halo_copies(up):
        out = []
        for i, h in enumerate((v_hbm, g_hbm)):
            out.append(pltpu.make_async_remote_copy(
                src_ref=h.at[0, 0] if up else h.at[0, rows - 1],
                dst_ref=halo.at[i, 1 if up else 0],
                send_sem=halo_send.at[i, 1 if up else 0],
                recv_sem=halo_recv.at[i, 1 if up else 0],
                device_id={"band": band - 1 if up else band + 1},
                device_id_type=MESH,
            ))
        return out

    @pl.when(band > 0)
    def _():
        for c in halo_copies(True):
            c.start()

    @pl.when(band < nb - 1)
    def _():
        for c in halo_copies(False):
            c.start()

    masks = {size: same_head(size) for _, size in groups(wide)}
    ones = {size: masks[size].astype(F32).astype(BF16) for size in masks}

    def put(src, at, size, compact, norm):
        for j in range(group):
            src[j, 0:share, at : at + size] = compact[share * j : share * (j + 1)]
            src[j, share : share + 1, at : at + size] = norm

    def spot(index):
        line = index % 16
        tile = index // 16
        return first + tile // per, line, (tile % per) * LANES

    def put_back(at, size, compact, norm):
        for t in range(size // LANES):
            tile = at // LANES + t
            lane = (tile % per) * LANES
            for h in range(2):
                stage[2 * (tile // per) + h, :, lane : lane + LANES] = compact[
                    16 * h : 16 * h + 16, t * LANES : (t + 1) * LANES]
            slot, line, lane = spot(tile)
            stage[slot, line : line + 1, lane : lane + LANES] = norm[
                :, t * LANES : (t + 1) * LANES]

    def phase1(way, src, r1):
        out = []
        for o in range(1, group):
            p, dev = peer_of(o)
            c = pltpu.make_async_remote_copy(
                src_ref=src.at[p], dst_ref=r1.at[m], send_sem=s1.at[way, o],
                recv_sem=v1.at[way, m], device_id=dev, device_id_type=MESH)
            c.start()
            out.append(c)
        r1[pl.ds(m, 1)] = src[pl.ds(m, 1)]
        return out

    def wait1(way, src, r1):
        for o in range(1, group):
            p, dev = peer_of(o)
            pltpu.make_async_remote_copy(
                src_ref=src.at[p], dst_ref=r1.at[p], send_sem=s1.at[way, o],
                recv_sem=v1.at[way, p], device_id=dev, device_id_type=MESH).wait_recv()

    def phase2(way, r1, tot, r2):
        total = r1[0].astype(F32)
        for j in range(1, group):
            total = total + r1[j].astype(F32)
        total = total.astype(tot.dtype)
        tot[...] = total
        out = []
        for o in range(1, no):
            zp, dev = outer_of(o)
            c = pltpu.make_async_remote_copy(
                src_ref=tot, dst_ref=r2.at[z], send_sem=s2.at[way, o],
                recv_sem=v2.at[way, z], device_id=dev, device_id_type=MESH)
            c.start()
            out.append(c)
        r2[pl.ds(z, 1)] = total[None]
        return out

    def wait2(way, tot, r2):
        for o in range(1, no):
            zp, dev = outer_of(o)
            pltpu.make_async_remote_copy(
                src_ref=tot, dst_ref=r2.at[zp], send_sem=s2.at[way, o],
                recv_sem=v2.at[way, zp], device_id=dev, device_id_type=MESH).wait_recv()

    def phase3(way, r1, r2, res, r3):
        backward = way == 1
        run = jnp.zeros(tot_f.shape if way == 0 else tot_b.shape, F32)
        whole = run
        for zz in range(no):
            part = r2[zz].astype(F32)
            earlier = (zz > z) if backward else (zz < z)
            run = run + jnp.where(earlier, part, 0.0)
            whole = whole + part
        if backward:
            line = lax.broadcasted_iota(jnp.int32, run.shape, 0)
            tile = lax.broadcasted_iota(jnp.int32, run.shape, 1) // LANES
            extra = ((m - first) * per + tile) * 16 + line >= tiles
        for aa in (range(inner - 1, -1, -1) if backward else range(inner)):
            for bb in range(nb):
                run = run + r1[aa * nb + bb].astype(F32)
            res[aa] = (jnp.where(extra, whole, run) if backward else run).astype(res.dtype)
        out = []
        for o in range(1, group):
            p, dev = peer_of(o)
            c = pltpu.make_async_remote_copy(
                src_ref=res.at[p // nb], dst_ref=r3.at[m], send_sem=s3.at[way, o],
                recv_sem=v3.at[way, m], device_id=dev, device_id_type=MESH)
            c.start()
            out.append(c)
        r3[pl.ds(m, 1)] = res[pl.ds(a, 1)]
        return out

    def wait3(way, res, r3):
        for o in range(1, group):
            p, dev = peer_of(o)
            pltpu.make_async_remote_copy(
                src_ref=res.at[p // nb], dst_ref=r3.at[p], send_sem=s3.at[way, o],
                recv_sem=v3.at[way, p], device_id=dev, device_id_type=MESH).wait_recv()
        if way == 0:
            for j in range(group):
                state[share * j : share * (j + 1), :] = r3[j, 0:share, :]
            return
        for tile in range(tiles):
            lane = (tile % per) * LANES
            for h in range(2):
                state[16 * h : 16 * h + 16, tile * LANES : (tile + 1) * LANES] = r3[
                    2 * (tile // per) + h, :, lane : lane + LANES].astype(F32)
        extra_s[...] = r3[first:group].astype(F32)

    sent = []
    loads[0].wait()
    kf[:, 0:cols, 0:width] = feature(k_raw[...].astype(F32)).astype(BF16)
    loads[1].wait()
    vpad[1 : rows + 1, 0:cols, 0:width] = v_raw[...].astype(F32)
    for at, size in groups(wide):
        kg = kf[:, :, at : at + size].reshape(count, size)
        vg = vpad[1 : rows + 1, :, at : at + size].reshape(count, size).astype(BF16)
        own = compress(mm_at(kg, vg), masks[size])
        norm = jnp.sum(kg.astype(F32), axis=0, keepdims=True)
        put(src_f, at, size, own, norm)
    sent += phase1(0, src_f, r1_f)
    loads[2].wait()
    qf[:, 0:cols, 0:width] = feature(q_raw[...].astype(F32)).astype(BF16)
    loads[3].wait()
    gpad[1 : rows + 1, 0:cols, 0:width] = g_raw[...].astype(F32)
    loads[4].wait()
    for i in range(3):
        for j in range(3):
            wpad[3 * i + j : 3 * i + j + 1, 0:width] = w_raw[i, j : j + 1, :]

    def conv(t):
        lanes = pl.ds(pl.multiple_of(t * LANES, LANES), LANES)
        vb = vpad[:, :, lanes]
        gb = gpad[:, :, lanes]
        vs = (pltpu.roll(vb, 1, 1), vb, pltpu.roll(vb, COLS - 1, 1))
        gs = (pltpu.roll(gb, 1, 1), gb, pltpu.roll(gb, COLS - 1, 1))
        own = gb[1 : rows + 1]
        lo = jnp.zeros((rows, COLS, LANES), F32)
        vl = lo
        for i in range(3):
            for j in range(3):
                w = wpad[3 * i + j : 3 * i + j + 1, lanes].reshape(1, 1, LANES)
                near = vs[j][i : i + rows]
                lo = lo + w * near
                vl = vl + w * gs[2 - j][2 - i : 2 - i + rows]
                term = jnp.sum(jnp.sum(own * near, axis=0), axis=0, keepdims=True)
                kterm[3 * i + j : 3 * i + j + 1, lanes] = term
        loc[:, :, lanes] = lo
        vloc[:, :, lanes] = vl

    half = (tiles + 1) // 2
    wait1(0, src_f, r1_f)
    sent += phase2(0, r1_f, tot_f, r2_f)

    @pl.when(band > 0)
    def _():
        for c in halo_copies(False):
            c.wait_recv()

    @pl.when(band < nb - 1)
    def _():
        for c in halo_copies(True):
            c.wait_recv()

    for i, pad in enumerate((vpad, gpad)):
        pad[0, 0:cols, 0:width] = halo[i, 0].astype(F32)
        pad[rows + 1, 0:cols, 0:width] = halo[i, 1].astype(F32)
    pl.loop(0, half)(conv)
    wait2(0, tot_f, r2_f)
    sent += phase3(0, r1_f, r2_f, res_f, r3_f)
    pl.loop(half, tiles)(conv)
    for r in range(9):
        for t in range(tiles):
            slot, line, lane = spot(tiles * (r + 1) + t)
            stage[slot, line : line + 1, lane : lane + LANES] = kterm[
                r : r + 1, t * LANES : (t + 1) * LANES]
    wait3(0, res_f, r3_f)
    blocks = []
    for at, size in groups(wide):
        mask, one = masks[size], ones[size]
        high, low = expand(state[:, at : at + size], mask)
        norm = r3_f[0, share : share + 1, at : at + size]
        blocks.append((high, low, norm))
        qg = qf[:, :, at : at + size].reshape(count, size)
        gg = gpad[1 : rows + 1, :, at : at + size].reshape(count, size)
        dh, dl = parts_of(qg.astype(F32) * norm)
        den = mm(dh, one) + mm(dl, one)
        num = mm(qg, high) + mm(qg, low)
        rden = 1.0 / den
        attn = num * rden
        th, tl = parts_of(gg * attn)
        dgw = -(mm(th, one) + mm(tl, one)) * rden
        sh, sl = parts_of(gg * rden)
        own = compress(mm_at(qg, sh) + mm_at(qg, sl), mask)
        put_back(at, size, own, jnp.sum(qg.astype(F32) * dgw, axis=0, keepdims=True))
        attn_s[:, at : at + size] = attn
        rden_s[:, at : at + size] = rden
        dgw_s[:, at : at + size] = dgw
    src_b[...] = stage[...].astype(BF16)
    sent += phase1(1, src_b, r1_b)
    mixed = (attn_s[...].reshape(rows, COLS, wide) + loc[...]).astype(BF16)
    mixed_ref[0] = mixed[:, 0:cols, 0:width]
    wait1(1, src_b, r1_b)
    sent += phase2(1, r1_b, tot_b, r2_b)
    for (at, size), (high, low, norm) in zip(groups(wide), blocks):
        gg = gpad[1 : rows + 1, :, at : at + size].reshape(count, size)
        sh, sl = parts_of(gg * rden_s[:, at : at + size])
        back = mm_bt(sh, high) + mm_bt(sh, low) + mm_bt(sl, high)
        attn_s[:, at : at + size] = back + dgw_s[:, at : at + size] * norm
    grad = attn_s[...].reshape(rows, COLS, wide)[:, 0:cols, 0:width]
    qg_ref[0] = (grad * slope(q_raw[...].astype(F32))).astype(BF16)
    wait2(1, tot_b, r2_b)
    sent += phase3(1, r1_b, r2_b, res_b, r3_b)
    wait3(1, res_b, r3_b)
    for at, size in groups(wide):
        high, low = expand(state[:, at : at + size], masks[size])
        lines = []
        for t in range(at // LANES, (at + size) // LANES):
            slot, line, lane = spot(t)
            lines.append(extra_s[slot - first, line : line + 1, lane : lane + LANES])
        norm = jnp.concatenate(lines, axis=1) if len(lines) > 1 else lines[0]
        kg = kf[:, :, at : at + size].reshape(count, size)
        vg = vpad[1 : rows + 1, :, at : at + size].reshape(count, size).astype(BF16)
        attn_s[:, at : at + size] = mm_bt(vg, high) + mm_bt(vg, low) + norm
        rden_s[:, at : at + size] = mm(kg, high) + mm(kg, low)
    grad = attn_s[...].reshape(rows, COLS, wide)[:, 0:cols, 0:width]
    kg_ref[0] = (grad * slope(k_raw[...].astype(F32))).astype(BF16)
    vgrad = (rden_s[...].reshape(rows, COLS, wide) + vloc[...]).astype(BF16)
    vg_ref[0] = vgrad[:, 0:cols, 0:width]
    tokens = lax.axis_size("tm") * nb * rows * cols
    for r in range(9):
        for t in range(tiles):
            slot, line, lane = spot(tiles * (r + 1) + t)
            size = min(LANES, width - t * LANES)
            term = extra_s[slot - first, line : line + 1, lane : lane + size]
            wg_ref[r // 3, r % 3 : r % 3 + 1, t * LANES : t * LANES + size] = term * (
                1.0 / math.sqrt(tokens))

    for c in sent:
        c.wait_send()

    @pl.when(band > 0)
    def _():
        for c in halo_copies(True):
            c.wait_send()

    @pl.when(band < nb - 1)
    def _():
        for c in halo_copies(False):
            c.wait_send()


def shards(query_input, key_input, value_input, cotangent, local_kernel_weight):
    _, rows, cols, width = query_input.shape
    wide = -(-width // LANES) * LANES
    frames, nb = lax.axis_size("tm"), lax.axis_size("band")
    inner = 4
    no = frames // inner
    group = nb * inner
    share = HEAD_DIM // group
    tiles = wide // LANES
    per = -(-tiles // (group // 2))
    first = 2 * -(-tiles // per)
    lanes = per * LANES
    count = rows * COLS
    cfg = (rows, cols, width, wide, nb, no, inner, per, first)
    raw = pltpu.VMEM((rows, cols, width), BF16)

    def buffers(r, lanes, kind):
        return [
            pltpu.VMEM((n, r, lanes) if n else (r, lanes), kind)
            for n in (group, group, 0, no, inner, group)
        ]

    tok = jax.ShapeDtypeStruct(query_input.shape, BF16)
    dma = pltpu.SemaphoreType.DMA
    vm = pl.BlockSpec(memory_space=pltpu.VMEM)
    made = pl.pallas_call(
        functools.partial(kernel, cfg),
        out_shape=(tok, tok, tok, tok, jax.ShapeDtypeStruct(local_kernel_weight.shape, F32)),
        in_specs=[pl.BlockSpec(memory_space=pltpu.HBM)] * 5,
        out_specs=[vm] * 5,
        scratch_shapes=[
            raw, raw, raw, raw,
            pltpu.VMEM((2, 2, cols, width), BF16),
            pltpu.VMEM((rows + 2, COLS, wide), F32), pltpu.VMEM((rows + 2, COLS, wide), F32),
            pltpu.VMEM((rows, COLS, wide), BF16), pltpu.VMEM((rows, COLS, wide), BF16),
            pltpu.VMEM((16, wide), F32),
            pltpu.VMEM((rows, COLS, wide), F32), pltpu.VMEM((rows, COLS, wide), F32),
            pltpu.VMEM((16, wide), F32),
            pltpu.VMEM((count, wide), F32), pltpu.VMEM((count, wide), F32),
            pltpu.VMEM((count, wide), F32),
            pltpu.VMEM((HEAD_DIM, wide), F32),
            pltpu.VMEM((group, 16, lanes), F32), pltpu.VMEM((group - first, 16, lanes), F32),
            pltpu.VMEM(local_kernel_weight.shape, F32),
            *buffers(share + 1, wide, F32), *buffers(16, lanes, BF16),
            dma((5,)), dma((2, 2)), dma((2, 2)),
            dma((2, group)), dma((2, group)), dma((2, no)), dma((2, no)),
            dma((2, group)), dma((2, group)),
        ],
        compiler_params=pltpu.CompilerParams(
            collective_id=0, has_side_effects=True, vmem_limit_bytes=62 * 1024 * 1024
        ),
        cost_estimate=pl.CostEstimate(flops=10**9, bytes_accessed=3 * 10**6, transcendentals=0),
        name="block_causal",
    )(query_input, key_input, value_input, cotangent, local_kernel_weight)
    return pl.pallas_call(
        hand_over,
        out_shape=tuple(jax.ShapeDtypeStruct(x.shape, x.dtype) for x in made),
        in_specs=[pl.BlockSpec(memory_space=pl.ANY)] * 5,
        out_specs=[pl.BlockSpec(memory_space=pltpu.HBM)] * 5,
        scratch_shapes=[dma((5,))],
        compiler_params=pltpu.CompilerParams(vmem_limit_bytes=62 * 1024 * 1024),
        name="hand_over",
    )(*made)


def hand_over(*refs):
    sems = refs[10]
    copies = [pltpu.make_async_copy(refs[i], refs[5 + i], sems.at[i]) for i in range(5)]
    for c in copies:
        c.start()
    for c in copies:
        c.wait()


def solution(mesh):
    token = P("tm", "band", None, None)
    return jax.shard_map(
        shards,
        mesh=mesh,
        in_specs=(token,) * 4 + (P(),),
        out_specs=(token,) * 4 + (P(),),
        check_vma=False,
    )
```

```python
import functools
import math

import jax
import jax.numpy as jnp
from jax import lax
from jax.experimental import pallas as pl
from jax.experimental.pallas import tpu as pltpu
from jax.sharding import PartitionSpec as P

HEAD_DIM = 32
LANES = 128
COLS = 32
MESH = pl.DeviceIdType.MESH
F32 = jnp.float32
BF16 = jnp.bfloat16


def groups(wide):
    out, at = [], 0
    while at < wide:
        size = min(256, wide - at)
        out.append((at, size))
        at += size
    return out


def feature(x):
    return jnp.where(x > 0, x + 1.0, jnp.exp(jnp.minimum(x, 0.0)))


def slope(x):
    return jnp.where(x > 0, 1.0, jnp.exp(jnp.minimum(x, 0.0)))


def parts_of(x):
    high = x.astype(BF16)
    return high, (x - high.astype(F32)).astype(BF16)


def mm(a, b):
    return lax.dot_general(a, b, (((1,), (0,)), ((), ())), preferred_element_type=F32)


def mm_bt(a, b):
    return lax.dot_general(a, b, (((1,), (1,)), ((), ())), preferred_element_type=F32)


def mm_at(a, b):
    return lax.dot_general(a, b, (((0,), (0,)), ((), ())), preferred_element_type=F32)


def same_head(size):
    row = lax.broadcasted_iota(jnp.int32, (size, size), 0) // HEAD_DIM
    lane = lax.broadcasted_iota(jnp.int32, (size, size), 1) // HEAD_DIM
    return row == lane


def compress(full, mask):
    size = full.shape[0]
    kept = jnp.where(mask, full, 0.0)
    total = kept[0:HEAD_DIM]
    for h in range(1, size // HEAD_DIM):
        total = total + kept[h * HEAD_DIM : (h + 1) * HEAD_DIM]
    return total


def expand(compact, mask):
    size = compact.shape[1]
    tiled = jnp.concatenate([compact] * (size // HEAD_DIM), axis=0)
    return parts_of(jnp.where(mask, tiled, 0.0))


def kernel(cfg, q_hbm, k_hbm, v_hbm, g_hbm, w_hbm, mixed_ref, qg_ref, kg_ref, vg_ref, wg_ref,
           q_raw, k_raw, v_raw, g_raw, halo, vpad, gpad, qf, kf, wpad, loc, vloc, kterm,
           attn_s, rden_s, dgw_s, state, stage, extra_s, w_raw, src_f, r1_f, tot_f, r2_f, res_f, r3_f,
           src_b, r1_b, tot_b, r2_b, res_b, r3_b,
           in_sem, halo_send, halo_recv, s1, v1, s2, v2, s3, v3):
    rows, cols, width, wide, nb, no, inner, per, first = cfg
    group = nb * inner
    count = rows * COLS
    tm = lax.axis_index("tm")
    band = lax.axis_index("band")
    z = tm // inner
    tiles = wide // LANES
    a = tm % inner
    m = a * nb + band

    def peer_of(o):
        p = (m + o) % group
        return p, {"tm": z * inner + p // nb, "band": p % nb}

    def outer_of(o):
        zp = (z + o) % no
        return zp, {"tm": zp * inner + a, "band": band}

    loads = [
        [pltpu.make_async_copy(h.at[0, r], d.at[r], in_sem.at[i, r]) for r in range(rows)]
        for i, (h, d) in enumerate(((k_hbm, k_raw), (v_hbm, v_raw), (q_hbm, q_raw), (g_hbm, g_raw)))
    ]
    loads.append([pltpu.make_async_copy(w_hbm, w_raw, in_sem.at[4, 0])])
    for some in loads:
        for c in some:
            c.start()

    def loaded(i):
        for c in loads[i]:
            c.wait()

    halo[...] = jnp.zeros_like(halo)
    barrier = pltpu.get_barrier_semaphore()
    for o in range(1, group):
        pl.semaphore_signal(barrier, inc=1, device_id=peer_of(o)[1], device_id_type=MESH)
    for o in range(1, no):
        pl.semaphore_signal(barrier, inc=1, device_id=outer_of(o)[1], device_id_type=MESH)

    vpad[...] = jnp.zeros_like(vpad)
    gpad[...] = jnp.zeros_like(gpad)
    kf[...] = jnp.zeros_like(kf)
    kf[:, 0:cols, width:wide] = jnp.ones((rows, cols, wide - width), BF16)
    qf[...] = jnp.ones_like(qf)
    wpad[...] = jnp.zeros_like(wpad)
    src_f[...] = jnp.zeros_like(src_f)
    stage[...] = jnp.zeros_like(stage)

    def halo_copies(up):
        out = []
        for i, h in enumerate((v_hbm, g_hbm)):
            out.append(pltpu.make_async_remote_copy(
                src_ref=h.at[0, 0] if up else h.at[0, rows - 1],
                dst_ref=halo.at[i, 1 if up else 0],
                send_sem=halo_send.at[i, 1 if up else 0],
                recv_sem=halo_recv.at[i, 1 if up else 0],
                device_id={"band": band - 1 if up else band + 1},
                device_id_type=MESH,
            ))
        return out

    masks = {size: same_head(size) for _, size in groups(wide)}
    ones = {size: masks[size].astype(F32).astype(BF16) for size in masks}

    def spot(index):
        line = index % 16
        tile = index // 16
        return first + tile // per, line, (tile % per) * LANES

    def put(dst, at, size, compact, norm):
        for t in range(size // LANES):
            tile = at // LANES + t
            lane = (tile % per) * LANES
            for h in range(2):
                dst[2 * (tile // per) + h, :, lane : lane + LANES] = compact[
                    16 * h : 16 * h + 16, t * LANES : (t + 1) * LANES]
            slot, line, lane = spot(tile)
            dst[slot, line : line + 1, lane : lane + LANES] = norm[
                :, t * LANES : (t + 1) * LANES]

    def phase1(way, src, r1):
        out = []
        for o in range(1, group):
            p, dev = peer_of(o)
            c = pltpu.make_async_remote_copy(
                src_ref=src.at[p], dst_ref=r1.at[m], send_sem=s1.at[way, o],
                recv_sem=v1.at[way, m], device_id=dev, device_id_type=MESH)
            c.start()
            out.append(c)
        r1[pl.ds(m, 1)] = src[pl.ds(m, 1)]
        return out

    def wait1(way, src, r1):
        for o in range(1, group):
            p, dev = peer_of(o)
            pltpu.make_async_remote_copy(
                src_ref=src.at[p], dst_ref=r1.at[p], send_sem=s1.at[way, o],
                recv_sem=v1.at[way, p], device_id=dev, device_id_type=MESH).wait_recv()

    def phase2(way, r1, tot, r2):
        total = r1[0].astype(F32)
        for j in range(1, group):
            total = total + r1[j].astype(F32)
        total = total.astype(tot.dtype)
        tot[...] = total
        out = []
        for o in range(1, no):
            zp, dev = outer_of(o)
            c = pltpu.make_async_remote_copy(
                src_ref=tot, dst_ref=r2.at[z], send_sem=s2.at[way, o],
                recv_sem=v2.at[way, z], device_id=dev, device_id_type=MESH)
            c.start()
            out.append(c)
        r2[pl.ds(z, 1)] = total[None]
        return out

    def wait2(way, tot, r2):
        for o in range(1, no):
            zp, dev = outer_of(o)
            pltpu.make_async_remote_copy(
                src_ref=tot, dst_ref=r2.at[zp], send_sem=s2.at[way, o],
                recv_sem=v2.at[way, zp], device_id=dev, device_id_type=MESH).wait_recv()

    def phase3(way, r1, r2, res, r3):
        backward = way == 1
        run = jnp.zeros(tot_f.shape if way == 0 else tot_b.shape, F32)
        whole = run
        for zz in range(no):
            part = r2[zz].astype(F32)
            earlier = (zz > z) if backward else (zz < z)
            run = run + jnp.where(earlier, part, 0.0)
            whole = whole + part
        if backward:
            line = lax.broadcasted_iota(jnp.int32, run.shape, 0)
            tile = lax.broadcasted_iota(jnp.int32, run.shape, 1) // LANES
            extra = ((m - first) * per + tile) * 16 + line >= tiles
        for aa in (range(inner - 1, -1, -1) if backward else range(inner)):
            for bb in range(nb):
                run = run + r1[aa * nb + bb].astype(F32)
            res[aa] = (jnp.where(extra, whole, run) if backward else run).astype(res.dtype)
        out = []
        for o in range(1, group):
            p, dev = peer_of(o)
            c = pltpu.make_async_remote_copy(
                src_ref=res.at[p // nb], dst_ref=r3.at[m], send_sem=s3.at[way, o],
                recv_sem=v3.at[way, m], device_id=dev, device_id_type=MESH)
            c.start()
            out.append(c)
        r3[pl.ds(m, 1)] = res[pl.ds(a, 1)]
        return out

    def wait3(way, res, r3):
        for o in range(1, group):
            p, dev = peer_of(o)
            pltpu.make_async_remote_copy(
                src_ref=res.at[p // nb], dst_ref=r3.at[p], send_sem=s3.at[way, o],
                recv_sem=v3.at[way, p], device_id=dev, device_id_type=MESH).wait_recv()
        for tile in range(tiles):
            lane = (tile % per) * LANES
            for h in range(2):
                state[16 * h : 16 * h + 16, tile * LANES : (tile + 1) * LANES] = r3[
                    2 * (tile // per) + h, :, lane : lane + LANES].astype(F32)
        extra_s[...] = r3[first:group].astype(F32)

    def norm_of(at, size):
        lines = []
        for t in range(at // LANES, (at + size) // LANES):
            slot, line, lane = spot(t)
            lines.append(extra_s[slot - first, line : line + 1, lane : lane + LANES])
        return jnp.concatenate(lines, axis=1) if len(lines) > 1 else lines[0]

    sent = []
    loaded(0)
    kf[:, 0:cols, 0:width] = feature(k_raw[...].astype(F32)).astype(BF16)
    loaded(1)
    vpad[1 : rows + 1, 0:cols, 0:width] = v_raw[...].astype(F32)
    for at, size in groups(wide):
        kg = kf[:, :, at : at + size].reshape(count, size)
        vg = vpad[1 : rows + 1, :, at : at + size].reshape(count, size).astype(BF16)
        own = compress(mm_at(kg, vg), masks[size])
        norm = jnp.sum(kg.astype(F32), axis=0, keepdims=True)
        put(src_f, at, size, own, norm)
    pl.semaphore_wait(barrier, group - 1 + no - 1)
    sent += phase1(0, src_f, r1_f)

    @pl.when(band > 0)
    def _():
        for c in halo_copies(True):
            c.start()

    @pl.when(band < nb - 1)
    def _():
        for c in halo_copies(False):
            c.start()

    loaded(2)
    qf[:, 0:cols, 0:width] = feature(q_raw[...].astype(F32)).astype(BF16)
    loaded(3)
    gpad[1 : rows + 1, 0:cols, 0:width] = g_raw[...].astype(F32)
    loaded(4)
    for i in range(3):
        for j in range(3):
            wpad[3 * i + j : 3 * i + j + 1, 0:width] = w_raw[i, j : j + 1, :]

    def conv(t):
        lanes = pl.ds(pl.multiple_of(t * LANES, LANES), LANES)
        vb = vpad[:, :, lanes]
        gb = gpad[:, :, lanes]
        vs = (pltpu.roll(vb, 1, 1), vb, pltpu.roll(vb, COLS - 1, 1))
        gs = (pltpu.roll(gb, 1, 1), gb, pltpu.roll(gb, COLS - 1, 1))
        own = gb[1 : rows + 1]
        lo = jnp.zeros((rows, COLS, LANES), F32)
        vl = lo
        for i in range(3):
            for j in range(3):
                w = wpad[3 * i + j : 3 * i + j + 1, lanes].reshape(1, 1, LANES)
                near = vs[j][i : i + rows]
                lo = lo + w * near
                vl = vl + w * gs[2 - j][2 - i : 2 - i + rows]
                term = jnp.sum(jnp.sum(own * near, axis=0), axis=0, keepdims=True)
                kterm[3 * i + j : 3 * i + j + 1, lanes] = term
        loc[:, :, lanes] = lo
        vloc[:, :, lanes] = vl

    half = (tiles + 1) // 2
    wait1(0, src_f, r1_f)
    sent += phase2(0, r1_f, tot_f, r2_f)

    @pl.when(band > 0)
    def _():
        for c in halo_copies(False):
            c.wait_recv()

    @pl.when(band < nb - 1)
    def _():
        for c in halo_copies(True):
            c.wait_recv()

    for i, pad in enumerate((vpad, gpad)):
        pad[0, 0:cols, 0:width] = halo[i, 0].astype(F32)
        pad[rows + 1, 0:cols, 0:width] = halo[i, 1].astype(F32)
    pl.loop(0, half)(conv)
    wait2(0, tot_f, r2_f)
    sent += phase3(0, r1_f, r2_f, res_f, r3_f)
    pl.loop(half, tiles)(conv)
    for r in range(9):
        for t in range(tiles):
            slot, line, lane = spot(tiles * (r + 1) + t)
            stage[slot, line : line + 1, lane : lane + LANES] = kterm[
                r : r + 1, t * LANES : (t + 1) * LANES]
    wait3(0, res_f, r3_f)
    blocks = []
    for at, size in groups(wide):
        mask, one = masks[size], ones[size]
        high, low = expand(state[:, at : at + size], mask)
        norm = norm_of(at, size)
        blocks.append((high, low, norm))
        qg = qf[:, :, at : at + size].reshape(count, size)
        gg = gpad[1 : rows + 1, :, at : at + size].reshape(count, size)
        dh, dl = parts_of(qg.astype(F32) * norm)
        den = mm(dh, one) + mm(dl, one)
        num = mm(qg, high) + mm(qg, low)
        rden = 1.0 / den
        attn = num * rden
        th, tl = parts_of(gg * attn)
        dgw = -(mm(th, one) + mm(tl, one)) * rden
        sh, sl = parts_of(gg * rden)
        own = compress(mm_at(qg, sh) + mm_at(qg, sl), mask)
        put(stage, at, size, own, jnp.sum(qg.astype(F32) * dgw, axis=0, keepdims=True))
        attn_s[:, at : at + size] = attn
        rden_s[:, at : at + size] = rden
        dgw_s[:, at : at + size] = dgw
    src_b[...] = stage[...].astype(BF16)
    sent += phase1(1, src_b, r1_b)
    mixed = (attn_s[...].reshape(rows, COLS, wide) + loc[...]).astype(BF16)
    mixed_ref[0] = mixed[:, 0:cols, 0:width]
    wait1(1, src_b, r1_b)
    sent += phase2(1, r1_b, tot_b, r2_b)
    for (at, size), (high, low, norm) in zip(groups(wide), blocks):
        gg = gpad[1 : rows + 1, :, at : at + size].reshape(count, size)
        sh, sl = parts_of(gg * rden_s[:, at : at + size])
        back = mm_bt(sh, high) + mm_bt(sh, low) + mm_bt(sl, high)
        attn_s[:, at : at + size] = back + dgw_s[:, at : at + size] * norm
    grad = attn_s[...].reshape(rows, COLS, wide)[:, 0:cols, 0:width]
    qg_ref[0] = (grad * slope(q_raw[...].astype(F32))).astype(BF16)
    wait2(1, tot_b, r2_b)
    sent += phase3(1, r1_b, r2_b, res_b, r3_b)
    wait3(1, res_b, r3_b)
    for at, size in groups(wide):
        high, low = expand(state[:, at : at + size], masks[size])
        norm = norm_of(at, size)
        kg = kf[:, :, at : at + size].reshape(count, size)
        vg = vpad[1 : rows + 1, :, at : at + size].reshape(count, size).astype(BF16)
        attn_s[:, at : at + size] = mm_bt(vg, high) + mm_bt(vg, low) + norm
        rden_s[:, at : at + size] = mm(kg, high) + mm(kg, low)
    grad = attn_s[...].reshape(rows, COLS, wide)[:, 0:cols, 0:width]
    kg_ref[0] = (grad * slope(k_raw[...].astype(F32))).astype(BF16)
    vgrad = (rden_s[...].reshape(rows, COLS, wide) + vloc[...]).astype(BF16)
    vg_ref[0] = vgrad[:, 0:cols, 0:width]
    tokens = lax.axis_size("tm") * nb * rows * cols
    for r in range(9):
        for t in range(tiles):
            slot, line, lane = spot(tiles * (r + 1) + t)
            size = min(LANES, width - t * LANES)
            term = extra_s[slot - first, line : line + 1, lane : lane + size]
            wg_ref[r // 3, r % 3 : r % 3 + 1, t * LANES : t * LANES + size] = term * (
                1.0 / math.sqrt(tokens))

    for c in sent:
        c.wait_send()

    @pl.when(band > 0)
    def _():
        for c in halo_copies(True):
            c.wait_send()

    @pl.when(band < nb - 1)
    def _():
        for c in halo_copies(False):
            c.wait_send()


def shards(query_input, key_input, value_input, cotangent, local_kernel_weight):
    _, rows, cols, width = query_input.shape
    wide = -(-width // LANES) * LANES
    frames, nb = lax.axis_size("tm"), lax.axis_size("band")
    inner = 4
    no = frames // inner
    group = nb * inner
    tiles = wide // LANES
    per = -(-tiles // (group // 2))
    first = 2 * -(-tiles // per)
    lanes = per * LANES
    count = rows * COLS
    cfg = (rows, cols, width, wide, nb, no, inner, per, first)
    raw = pltpu.VMEM((rows, cols, width), BF16)

    def buffers(r, lanes, kind):
        return [
            pltpu.VMEM((n, r, lanes) if n else (r, lanes), kind)
            for n in (group, group, 0, no, inner, group)
        ]

    tok = jax.ShapeDtypeStruct(query_input.shape, BF16)
    dma = pltpu.SemaphoreType.DMA
    vm = pl.BlockSpec(memory_space=pltpu.VMEM)
    made = pl.pallas_call(
        functools.partial(kernel, cfg),
        out_shape=(tok, tok, tok, tok, jax.ShapeDtypeStruct(local_kernel_weight.shape, F32)),
        in_specs=[pl.BlockSpec(memory_space=pltpu.HBM)] * 5,
        out_specs=[vm] * 5,
        scratch_shapes=[
            raw, raw, raw, raw,
            pltpu.VMEM((2, 2, cols, width), BF16),
            pltpu.VMEM((rows + 2, COLS, wide), F32), pltpu.VMEM((rows + 2, COLS, wide), F32),
            pltpu.VMEM((rows, COLS, wide), BF16), pltpu.VMEM((rows, COLS, wide), BF16),
            pltpu.VMEM((16, wide), F32),
            pltpu.VMEM((rows, COLS, wide), F32), pltpu.VMEM((rows, COLS, wide), F32),
            pltpu.VMEM((16, wide), F32),
            pltpu.VMEM((count, wide), F32), pltpu.VMEM((count, wide), F32),
            pltpu.VMEM((count, wide), F32),
            pltpu.VMEM((HEAD_DIM, wide), F32),
            pltpu.VMEM((group, 16, lanes), F32), pltpu.VMEM((group - first, 16, lanes), F32),
            pltpu.VMEM(local_kernel_weight.shape, F32),
            *buffers(16, lanes, F32), *buffers(16, lanes, BF16),
            dma((5, rows)), dma((2, 2)), dma((2, 2)),
            dma((2, group)), dma((2, group)), dma((2, no)), dma((2, no)),
            dma((2, group)), dma((2, group)),
        ],
        compiler_params=pltpu.CompilerParams(
            collective_id=0, has_side_effects=True, vmem_limit_bytes=62 * 1024 * 1024
        ),
        cost_estimate=pl.CostEstimate(flops=10**9, bytes_accessed=3 * 10**6, transcendentals=0),
        name="block_causal",
    )(query_input, key_input, value_input, cotangent, local_kernel_weight)
    return pl.pallas_call(
        hand_over,
        out_shape=tuple(jax.ShapeDtypeStruct(x.shape, x.dtype) for x in made),
        in_specs=[pl.BlockSpec(memory_space=pl.ANY)] * 5,
        out_specs=[pl.BlockSpec(memory_space=pltpu.HBM)] * 5,
        scratch_shapes=[pltpu.VMEM(x.shape, x.dtype) for x in made]
        + [dma((5, rows)), dma((5, rows))],
        compiler_params=pltpu.CompilerParams(vmem_limit_bytes=62 * 1024 * 1024),
        name="hand_over",
    )(*made)


def hand_over(*refs):
    pieces = []
    for i in range(5):
        src, dst, held = refs[i], refs[5 + i], refs[10 + i]
        steps = range(src.shape[1]) if i < 4 else (None,)
        for r in steps:
            at = (lambda x, r=r: x if r is None else x.at[0, r])
            n = 0 if r is None else r
            pieces.append((
                pltpu.make_async_copy(at(src), at(held), refs[15].at[i, n]),
                pltpu.make_async_copy(at(held), at(dst), refs[16].at[i, n]),
            ))
    for load, _ in pieces:
        load.start()
    for load, store in pieces:
        load.wait()
        store.start()
    for _, store in pieces:
        store.wait()


def solution(mesh):
    token = P("tm", "band", None, None)
    return jax.shard_map(
        shards,
        mesh=mesh,
        in_specs=(token,) * 4 + (P(),),
        out_specs=(token,) * 4 + (P(),),
        check_vma=False,
    )
```

```python
import functools
import math

import jax
import jax.numpy as jnp
from jax import lax
from jax.experimental import pallas as pl
from jax.experimental.pallas import tpu as pltpu
from jax.sharding import PartitionSpec as P

HEAD_DIM = 32
LANES = 128
COLS = 32
MESH = pl.DeviceIdType.MESH
F32 = jnp.float32
BF16 = jnp.bfloat16


def groups(wide):
    out, at = [], 0
    while at < wide:
        size = min(256, wide - at)
        out.append((at, size))
        at += size
    return out


def feature(x):
    return jnp.where(x > 0, x + 1.0, jnp.exp(jnp.minimum(x, 0.0)))


def slope(x):
    return jnp.where(x > 0, 1.0, jnp.exp(jnp.minimum(x, 0.0)))


def parts_of(x):
    high = x.astype(BF16)
    return high, (x - high.astype(F32)).astype(BF16)


def mm(a, b):
    return lax.dot_general(a, b, (((1,), (0,)), ((), ())), preferred_element_type=F32)


def mm_bt(a, b):
    return lax.dot_general(a, b, (((1,), (1,)), ((), ())), preferred_element_type=F32)


def mm_at(a, b):
    return lax.dot_general(a, b, (((0,), (0,)), ((), ())), preferred_element_type=F32)


def same_head(size):
    row = lax.broadcasted_iota(jnp.int32, (size, size), 0) // HEAD_DIM
    lane = lax.broadcasted_iota(jnp.int32, (size, size), 1) // HEAD_DIM
    return row == lane


def compress(full, mask):
    size = full.shape[0]
    kept = jnp.where(mask, full, 0.0)
    total = kept[0:HEAD_DIM]
    for h in range(1, size // HEAD_DIM):
        total = total + kept[h * HEAD_DIM : (h + 1) * HEAD_DIM]
    return total


def expand(compact, mask):
    size = compact.shape[1]
    tiled = jnp.concatenate([compact] * (size // HEAD_DIM), axis=0)
    return parts_of(jnp.where(mask, tiled, 0.0))


def kernel(cfg, q_hbm, k_hbm, v_hbm, g_hbm, w_hbm, mixed_ref, qg_ref, kg_ref, vg_ref, wg_ref,
           q_raw, k_raw, v_raw, g_raw, mixed_out, qg_out, kg_out, vg_out, wg_out, out_sem, halo, vpad, gpad, qf, kf, wpad, loc, vloc, kterm,
           attn_s, rden_s, dgw_s, state, stage, extra_s, w_raw, src_f, r1_f, tot_f, r2_f, res_f, r3_f,
           src_b, r1_b, tot_b, r2_b, res_b, r3_b,
           in_sem, halo_send, halo_recv, s1, v1, s2, v2, s3, v3):
    rows, cols, width, wide, nb, no, inner, per, first, fper = cfg
    group = nb * inner
    count = rows * COLS
    tm = lax.axis_index("tm")
    band = lax.axis_index("band")
    z = tm // inner
    tiles = wide // LANES
    a = tm % inner
    m = a * nb + band

    def peer_of(o):
        p = (m + o) % group
        return p, {"tm": z * inner + p // nb, "band": p % nb}

    def outer_of(o):
        zp = (z + o) % no
        return zp, {"tm": zp * inner + a, "band": band}

    loads = [
        [pltpu.make_async_copy(h.at[0, r], d.at[r], in_sem.at[i, r]) for r in range(rows)]
        for i, (h, d) in enumerate(((k_hbm, k_raw), (v_hbm, v_raw), (q_hbm, q_raw), (g_hbm, g_raw)))
    ]
    loads.append([pltpu.make_async_copy(w_hbm, w_raw, in_sem.at[4, 0])])
    for some in loads:
        for c in some:
            c.start()

    def loaded(i):
        for c in loads[i]:
            c.wait()

    halo[...] = jnp.zeros_like(halo)
    barrier = pltpu.get_barrier_semaphore()
    for o in range(1, group):
        pl.semaphore_signal(barrier, inc=1, device_id=peer_of(o)[1], device_id_type=MESH)
    for o in range(1, no):
        pl.semaphore_signal(barrier, inc=1, device_id=outer_of(o)[1], device_id_type=MESH)

    vpad[...] = jnp.zeros_like(vpad)
    gpad[...] = jnp.zeros_like(gpad)
    kf[...] = jnp.zeros_like(kf)
    kf[:, 0:cols, width:wide] = jnp.ones((rows, cols, wide - width), BF16)
    qf[...] = jnp.ones_like(qf)
    wpad[...] = jnp.zeros_like(wpad)
    src_f[...] = jnp.zeros_like(src_f)
    stage[...] = jnp.zeros_like(stage)

    def halo_copies(up):
        out = []
        for i, h in enumerate((v_hbm, g_hbm)):
            out.append(pltpu.make_async_remote_copy(
                src_ref=h.at[0, 0] if up else h.at[0, rows - 1],
                dst_ref=halo.at[i, 1 if up else 0],
                send_sem=halo_send.at[i, 1 if up else 0],
                recv_sem=halo_recv.at[i, 1 if up else 0],
                device_id={"band": band - 1 if up else band + 1},
                device_id_type=MESH,
            ))
        return out

    masks = {size: same_head(size) for _, size in groups(wide)}
    ones = {size: masks[size].astype(F32).astype(BF16) for size in masks}

    def spot(index):
        line = index % 16
        tile = index // 16
        return first + tile // per, line, (tile % per) * LANES

    def put(dst, at, size, compact, norm):
        for t in range(size // LANES):
            tile = at // LANES + t
            lane = (tile % per) * LANES
            for h in range(2):
                dst[2 * (tile // per) + h, :, lane : lane + LANES] = compact[
                    16 * h : 16 * h + 16, t * LANES : (t + 1) * LANES]
            slot, line, lane = spot(tile)
            dst[slot, line : line + 1, lane : lane + LANES] = norm[
                :, t * LANES : (t + 1) * LANES]

    def put_forward(at, size, compact, norm):
        for t in range(size // LANES):
            tile = at // LANES + t
            part = slice(t * LANES, (t + 1) * LANES)
            for h in range(4):
                slot, lane = (4 * tile + h) // fper, (4 * tile + h) % fper * LANES
                src_f[slot, :, lane : lane + LANES] = compact[8 * h : 8 * h + 8, part]
            piece = 4 * tiles + tile // 8
            slot, lane, line = piece // fper, piece % fper * LANES, tile % 8
            src_f[slot, line : line + 1, lane : lane + LANES] = norm[:, part]

    def norm_forward(at, size):
        lines = []
        for tile in range(at // LANES, (at + size) // LANES):
            piece = 4 * tiles + tile // 8
            slot, lane, line = piece // fper, piece % fper * LANES, tile % 8
            lines.append(r3_f[slot, line : line + 1, lane : lane + LANES])
        return jnp.concatenate(lines, axis=1) if len(lines) > 1 else lines[0]

    def phase1(way, src, r1):
        out = []
        for o in range(1, group):
            p, dev = peer_of(o)
            c = pltpu.make_async_remote_copy(
                src_ref=src.at[p], dst_ref=r1.at[m], send_sem=s1.at[way, o],
                recv_sem=v1.at[way, m], device_id=dev, device_id_type=MESH)
            c.start()
            out.append(c)
        r1[pl.ds(m, 1)] = src[pl.ds(m, 1)]
        return out

    def wait1(way, src, r1):
        for o in range(1, group):
            p, dev = peer_of(o)
            pltpu.make_async_remote_copy(
                src_ref=src.at[p], dst_ref=r1.at[p], send_sem=s1.at[way, o],
                recv_sem=v1.at[way, p], device_id=dev, device_id_type=MESH).wait_recv()

    def phase2(way, r1, tot, r2):
        total = r1[0].astype(F32)
        for j in range(1, group):
            total = total + r1[j].astype(F32)
        total = total.astype(tot.dtype)
        tot[...] = total
        out = []
        for o in range(1, no):
            zp, dev = outer_of(o)
            c = pltpu.make_async_remote_copy(
                src_ref=tot, dst_ref=r2.at[z], send_sem=s2.at[way, o],
                recv_sem=v2.at[way, z], device_id=dev, device_id_type=MESH)
            c.start()
            out.append(c)
        r2[pl.ds(z, 1)] = total[None]
        return out

    def wait2(way, tot, r2):
        for o in range(1, no):
            zp, dev = outer_of(o)
            pltpu.make_async_remote_copy(
                src_ref=tot, dst_ref=r2.at[zp], send_sem=s2.at[way, o],
                recv_sem=v2.at[way, zp], device_id=dev, device_id_type=MESH).wait_recv()

    def phase3(way, r1, r2, res, r3):
        backward = way == 1
        run = jnp.zeros(tot_f.shape if way == 0 else tot_b.shape, F32)
        whole = run
        for zz in range(no):
            part = r2[zz].astype(F32)
            earlier = (zz > z) if backward else (zz < z)
            run = run + jnp.where(earlier, part, 0.0)
            whole = whole + part
        if backward:
            line = lax.broadcasted_iota(jnp.int32, run.shape, 0)
            tile = lax.broadcasted_iota(jnp.int32, run.shape, 1) // LANES
            extra = ((m - first) * per + tile) * 16 + line >= tiles
        for aa in (range(inner - 1, -1, -1) if backward else range(inner)):
            for bb in range(nb):
                run = run + r1[aa * nb + bb].astype(F32)
            res[aa] = (jnp.where(extra, whole, run) if backward else run).astype(res.dtype)
        out = []
        for o in range(1, group):
            p, dev = peer_of(o)
            c = pltpu.make_async_remote_copy(
                src_ref=res.at[p // nb], dst_ref=r3.at[m], send_sem=s3.at[way, o],
                recv_sem=v3.at[way, m], device_id=dev, device_id_type=MESH)
            c.start()
            out.append(c)
        r3[pl.ds(m, 1)] = res[pl.ds(a, 1)]
        return out

    def wait3(way, res, r3):
        for o in range(1, group):
            p, dev = peer_of(o)
            pltpu.make_async_remote_copy(
                src_ref=res.at[p // nb], dst_ref=r3.at[p], send_sem=s3.at[way, o],
                recv_sem=v3.at[way, p], device_id=dev, device_id_type=MESH).wait_recv()
        if way == 0:
            for tile in range(tiles):
                for h in range(4):
                    slot, lane = (4 * tile + h) // fper, (4 * tile + h) % fper * LANES
                    state[8 * h : 8 * h + 8, tile * LANES : (tile + 1) * LANES] = r3[
                        slot, :, lane : lane + LANES]
            return
        for tile in range(tiles):
            lane = (tile % per) * LANES
            for h in range(2):
                state[16 * h : 16 * h + 16, tile * LANES : (tile + 1) * LANES] = r3[
                    2 * (tile // per) + h, :, lane : lane + LANES].astype(F32)
        extra_s[...] = r3[first:group].astype(F32)

    def norm_of(at, size):
        lines = []
        for t in range(at // LANES, (at + size) // LANES):
            slot, line, lane = spot(t)
            lines.append(extra_s[slot - first, line : line + 1, lane : lane + LANES])
        return jnp.concatenate(lines, axis=1) if len(lines) > 1 else lines[0]

    outs = ((mixed_out, mixed_ref), (qg_out, qg_ref), (kg_out, kg_ref), (vg_out, vg_ref))

    def writes(n):
        held, ref = outs[n]
        return [
            pltpu.make_async_copy(held.at[r], ref.at[0, r], out_sem.at[n, r]) for r in range(rows)
        ]

    def write(n):
        for c in writes(n):
            c.start()

    sent = []
    loaded(0)
    kf[:, 0:cols, 0:width] = feature(k_raw[...].astype(F32)).astype(BF16)
    loaded(1)
    vpad[1 : rows + 1, 0:cols, 0:width] = v_raw[...].astype(F32)
    for at, size in groups(wide):
        kg = kf[:, :, at : at + size].reshape(count, size)
        vg = vpad[1 : rows + 1, :, at : at + size].reshape(count, size).astype(BF16)
        own = compress(mm_at(kg, vg), masks[size])
        norm = jnp.sum(kg.astype(F32), axis=0, keepdims=True)
        put_forward(at, size, own, norm)
    pl.semaphore_wait(barrier, group - 1 + no - 1)
    sent += phase1(0, src_f, r1_f)

    @pl.when(band > 0)
    def _():
        for c in halo_copies(True):
            c.start()

    @pl.when(band < nb - 1)
    def _():
        for c in halo_copies(False):
            c.start()

    loaded(2)
    qf[:, 0:cols, 0:width] = feature(q_raw[...].astype(F32)).astype(BF16)
    loaded(3)
    gpad[1 : rows + 1, 0:cols, 0:width] = g_raw[...].astype(F32)
    loaded(4)
    for i in range(3):
        for j in range(3):
            wpad[3 * i + j : 3 * i + j + 1, 0:width] = w_raw[i, j : j + 1, :]

    def conv(t):
        lanes = pl.ds(pl.multiple_of(t * LANES, LANES), LANES)
        vb = vpad[:, :, lanes]
        gb = gpad[:, :, lanes]
        vs = (pltpu.roll(vb, 1, 1), vb, pltpu.roll(vb, COLS - 1, 1))
        gs = (pltpu.roll(gb, 1, 1), gb, pltpu.roll(gb, COLS - 1, 1))
        own = gb[1 : rows + 1]
        lo = jnp.zeros((rows, COLS, LANES), F32)
        vl = lo
        for i in range(3):
            for j in range(3):
                w = wpad[3 * i + j : 3 * i + j + 1, lanes].reshape(1, 1, LANES)
                near = vs[j][i : i + rows]
                lo = lo + w * near
                vl = vl + w * gs[2 - j][2 - i : 2 - i + rows]
                term = jnp.sum(jnp.sum(own * near, axis=0), axis=0, keepdims=True)
                kterm[3 * i + j : 3 * i + j + 1, lanes] = term
        loc[:, :, lanes] = lo
        vloc[:, :, lanes] = vl

    half = (tiles + 1) // 2
    wait1(0, src_f, r1_f)
    sent += phase2(0, r1_f, tot_f, r2_f)

    @pl.when(band > 0)
    def _():
        for c in halo_copies(False):
            c.wait_recv()

    @pl.when(band < nb - 1)
    def _():
        for c in halo_copies(True):
            c.wait_recv()

    for i, pad in enumerate((vpad, gpad)):
        pad[0, 0:cols, 0:width] = halo[i, 0].astype(F32)
        pad[rows + 1, 0:cols, 0:width] = halo[i, 1].astype(F32)
    pl.loop(0, half)(conv)
    wait2(0, tot_f, r2_f)
    sent += phase3(0, r1_f, r2_f, res_f, r3_f)
    pl.loop(half, tiles)(conv)
    for r in range(9):
        for t in range(tiles):
            slot, line, lane = spot(tiles * (r + 1) + t)
            stage[slot, line : line + 1, lane : lane + LANES] = kterm[
                r : r + 1, t * LANES : (t + 1) * LANES]
    wait3(0, res_f, r3_f)
    blocks = []
    for at, size in groups(wide):
        mask, one = masks[size], ones[size]
        high, low = expand(state[:, at : at + size], mask)
        norm = norm_forward(at, size)
        blocks.append((high, low, norm))
        qg = qf[:, :, at : at + size].reshape(count, size)
        gg = gpad[1 : rows + 1, :, at : at + size].reshape(count, size)
        dh, dl = parts_of(qg.astype(F32) * norm)
        den = mm(dh, one) + mm(dl, one)
        num = mm(qg, high) + mm(qg, low)
        rden = 1.0 / den
        attn = num * rden
        th, tl = parts_of(gg * attn)
        dgw = -(mm(th, one) + mm(tl, one)) * rden
        sh, sl = parts_of(gg * rden)
        own = compress(mm_at(qg, sh) + mm_at(qg, sl), mask)
        put(stage, at, size, own, jnp.sum(qg.astype(F32) * dgw, axis=0, keepdims=True))
        attn_s[:, at : at + size] = attn
        rden_s[:, at : at + size] = rden
        dgw_s[:, at : at + size] = dgw
    src_b[...] = stage[...].astype(BF16)
    sent += phase1(1, src_b, r1_b)
    mixed = (attn_s[...].reshape(rows, COLS, wide) + loc[...]).astype(BF16)
    mixed_out[...] = mixed[:, 0:cols, 0:width]
    write(0)
    wait1(1, src_b, r1_b)
    sent += phase2(1, r1_b, tot_b, r2_b)
    for (at, size), (high, low, norm) in zip(groups(wide), blocks):
        gg = gpad[1 : rows + 1, :, at : at + size].reshape(count, size)
        sh, sl = parts_of(gg * rden_s[:, at : at + size])
        back = mm_bt(sh, high) + mm_bt(sh, low) + mm_bt(sl, high)
        attn_s[:, at : at + size] = back + dgw_s[:, at : at + size] * norm
    grad = attn_s[...].reshape(rows, COLS, wide)[:, 0:cols, 0:width]
    qg_out[...] = (grad * slope(q_raw[...].astype(F32))).astype(BF16)
    write(1)
    wait2(1, tot_b, r2_b)
    sent += phase3(1, r1_b, r2_b, res_b, r3_b)
    steep = slope(k_raw[...].astype(F32))
    dgw_s[...] = jnp.ones_like(dgw_s)
    for r in range(rows):
        dgw_s[r * COLS : r * COLS + cols, 0:width] = steep[r]
    wait3(1, res_b, r3_b)
    for at, size in groups(wide):
        high, low = expand(state[:, at : at + size], masks[size])
        norm = norm_of(at, size)
        kg = kf[:, :, at : at + size].reshape(count, size)
        vg = vpad[1 : rows + 1, :, at : at + size].reshape(count, size).astype(BF16)
        back = mm_bt(vg, high) + mm_bt(vg, low) + norm
        attn_s[:, at : at + size] = back * dgw_s[:, at : at + size]
        rden_s[:, at : at + size] = mm(kg, high) + mm(kg, low) + vloc[
            :, :, at : at + size].reshape(count, size)
    for n, held, made in ((2, kg_out, attn_s), (3, vg_out, rden_s)):
        held[...] = made[...].reshape(rows, COLS, wide)[:, 0:cols, 0:width].astype(BF16)
        write(n)
    tokens = lax.axis_size("tm") * nb * rows * cols
    for r in range(9):
        for t in range(tiles):
            slot, line, lane = spot(tiles * (r + 1) + t)
            size = min(LANES, width - t * LANES)
            term = extra_s[slot - first, line : line + 1, lane : lane + size]
            wg_out[r // 3, r % 3 : r % 3 + 1, t * LANES : t * LANES + size] = term * (
                1.0 / math.sqrt(tokens))

    pltpu.make_async_copy(wg_out, wg_ref, out_sem.at[4, 0]).start()
    for n in range(4):
        for c in writes(n):
            c.wait()
    pltpu.make_async_copy(wg_out, wg_ref, out_sem.at[4, 0]).wait()
    for c in sent:
        c.wait_send()

    @pl.when(band > 0)
    def _():
        for c in halo_copies(True):
            c.wait_send()

    @pl.when(band < nb - 1)
    def _():
        for c in halo_copies(False):
            c.wait_send()


def shards(query_input, key_input, value_input, cotangent, local_kernel_weight):
    _, rows, cols, width = query_input.shape
    wide = -(-width // LANES) * LANES
    frames, nb = lax.axis_size("tm"), lax.axis_size("band")
    inner = 4
    no = frames // inner
    group = nb * inner
    tiles = wide // LANES
    per = -(-tiles // (group // 2))
    first = 2 * -(-tiles // per)
    lanes = per * LANES
    fper = -(-(4 * tiles + -(-tiles // 8)) // group)
    count = rows * COLS
    cfg = (rows, cols, width, wide, nb, no, inner, per, first, fper)
    raw = pltpu.VMEM((rows, cols, width), BF16)

    def buffers(r, lanes, kind):
        return [
            pltpu.VMEM((n, r, lanes) if n else (r, lanes), kind)
            for n in (group, group, 0, no, inner, group)
        ]

    tok = jax.ShapeDtypeStruct(query_input.shape, BF16)
    dma = pltpu.SemaphoreType.DMA
    made = pl.pallas_call(
        functools.partial(kernel, cfg),
        out_shape=(tok, tok, tok, tok, jax.ShapeDtypeStruct(local_kernel_weight.shape, F32)),
        in_specs=[pl.BlockSpec(memory_space=pltpu.HBM)] * 5,
        out_specs=[pl.BlockSpec(memory_space=pl.ANY)] * 5,
        scratch_shapes=[
            raw, raw, raw, raw, raw, raw, raw, raw,
            pltpu.VMEM(local_kernel_weight.shape, F32), dma((5, rows)),
            pltpu.VMEM((2, 2, cols, width), BF16),
            pltpu.VMEM((rows + 2, COLS, wide), F32), pltpu.VMEM((rows + 2, COLS, wide), F32),
            pltpu.VMEM((rows, COLS, wide), BF16), pltpu.VMEM((rows, COLS, wide), BF16),
            pltpu.VMEM((16, wide), F32),
            pltpu.VMEM((rows, COLS, wide), F32), pltpu.VMEM((rows, COLS, wide), F32),
            pltpu.VMEM((16, wide), F32),
            pltpu.VMEM((count, wide), F32), pltpu.VMEM((count, wide), F32),
            pltpu.VMEM((count, wide), F32),
            pltpu.VMEM((HEAD_DIM, wide), F32),
            pltpu.VMEM((group, 16, lanes), F32), pltpu.VMEM((group - first, 16, lanes), F32),
            pltpu.VMEM(local_kernel_weight.shape, F32),
            *buffers(8, fper * LANES, F32), *buffers(16, lanes, BF16),
            dma((5, rows)), dma((2, 2)), dma((2, 2)),
            dma((2, group)), dma((2, group)), dma((2, no)), dma((2, no)),
            dma((2, group)), dma((2, group)),
        ],
        compiler_params=pltpu.CompilerParams(
            collective_id=0, has_side_effects=True, vmem_limit_bytes=62 * 1024 * 1024
        ),
        cost_estimate=pl.CostEstimate(flops=10**9, bytes_accessed=3 * 10**6, transcendentals=0),
        name="block_causal",
    )(query_input, key_input, value_input, cotangent, local_kernel_weight)
    return pl.pallas_call(
        hand_over,
        out_shape=tuple(jax.ShapeDtypeStruct(x.shape, x.dtype) for x in made),
        in_specs=[pl.BlockSpec(memory_space=pl.ANY)] * 5,
        out_specs=[pl.BlockSpec(memory_space=pltpu.HBM)] * 5,
        scratch_shapes=[pltpu.VMEM(x.shape, x.dtype) for x in made]
        + [dma((5, rows)), dma((5, rows))],
        compiler_params=pltpu.CompilerParams(vmem_limit_bytes=62 * 1024 * 1024),
        name="hand_over",
    )(*made)


def hand_over(*refs):
    pieces = []
    for i in range(5):
        src, dst, held = refs[i], refs[5 + i], refs[10 + i]
        steps = range(src.shape[1]) if i < 4 else (None,)
        for r in steps:
            at = (lambda x, r=r: x if r is None else x.at[0, r])
            n = 0 if r is None else r
            pieces.append((
                pltpu.make_async_copy(at(src), at(held), refs[15].at[i, n]),
                pltpu.make_async_copy(at(held), at(dst), refs[16].at[i, n]),
            ))
    for load, _ in pieces:
        load.start()
    for load, store in pieces:
        load.wait()
        store.start()
    for _, store in pieces:
        store.wait()


def solution(mesh):
    token = P("tm", "band", None, None)
    return jax.shard_map(
        shards,
        mesh=mesh,
        in_specs=(token,) * 4 + (P(),),
        out_specs=(token,) * 4 + (P(),),
        check_vma=False,
    )
```

```python
import functools
import math

import jax
import jax.numpy as jnp
from jax import lax
from jax.experimental import pallas as pl
from jax.experimental.pallas import tpu as pltpu
from jax.sharding import PartitionSpec as P

HEAD_DIM = 32
LANES = 128
COLS = 32
MESH = pl.DeviceIdType.MESH
F32 = jnp.float32
BF16 = jnp.bfloat16


def groups(wide):
    out, at = [], 0
    while at < wide:
        size = min(256, wide - at)
        out.append((at, size))
        at += size
    return out


def feature(x):
    return jnp.where(x > 0, x + 1.0, jnp.exp(jnp.minimum(x, 0.0)))


def slope(x):
    return jnp.where(x > 0, 1.0, jnp.exp(jnp.minimum(x, 0.0)))


def parts_of(x):
    high = x.astype(BF16)
    return high, (x - high.astype(F32)).astype(BF16)


def mm(a, b):
    return lax.dot_general(a, b, (((1,), (0,)), ((), ())), preferred_element_type=F32)


def mm_bt(a, b):
    return lax.dot_general(a, b, (((1,), (1,)), ((), ())), preferred_element_type=F32)


def mm_at(a, b):
    return lax.dot_general(a, b, (((0,), (0,)), ((), ())), preferred_element_type=F32)


def same_head(size):
    row = lax.broadcasted_iota(jnp.int32, (size, size), 0) // HEAD_DIM
    lane = lax.broadcasted_iota(jnp.int32, (size, size), 1) // HEAD_DIM
    return row == lane


def compress(full, mask):
    size = full.shape[0]
    kept = jnp.where(mask, full, 0.0)
    total = kept[0:HEAD_DIM]
    for h in range(1, size // HEAD_DIM):
        total = total + kept[h * HEAD_DIM : (h + 1) * HEAD_DIM]
    return total


def expand(compact, mask):
    size = compact.shape[1]
    tiled = jnp.concatenate([compact] * (size // HEAD_DIM), axis=0)
    return parts_of(jnp.where(mask, tiled, 0.0))


def kernel(cfg, q_hbm, k_hbm, v_hbm, g_hbm, w_hbm, mixed_ref, qg_ref, kg_ref, vg_ref, wg_ref,
           q_raw, k_raw, v_raw, g_raw, mixed_out, qg_out, kg_out, vg_out, wg_out, out_sem, halo, vpad, gpad, qf, kf, wpad, loc, vloc, kterm,
           attn_s, rden_s, dgw_s, state, stage, extra_s, w_raw, src_f, r1_f, tot_f, r2_f, res_f, r3_f,
           src_b, r1_b, tot_b, r2_b, res_b, r3_b,
           in_sem, halo_send, halo_recv, s1, v1, s2, v2, s3, v3):
    rows, cols, width, wide, nb, no, inner, per, first, fper = cfg
    group = nb * inner
    count = rows * COLS
    tm = lax.axis_index("tm")
    band = lax.axis_index("band")
    z = tm // inner
    tiles = wide // LANES
    a = tm % inner
    m = a * nb + band

    def peer_of(o):
        p = (m + o) % group
        return p, {"tm": z * inner + p // nb, "band": p % nb}

    def outer_of(o):
        zp = (z + o) % no
        return zp, {"tm": zp * inner + a, "band": band}

    loads = [
        [pltpu.make_async_copy(h.at[0, r], d.at[r], in_sem.at[i, r]) for r in range(rows)]
        for i, (h, d) in enumerate(((k_hbm, k_raw), (v_hbm, v_raw), (q_hbm, q_raw), (g_hbm, g_raw)))
    ]
    loads.append([pltpu.make_async_copy(w_hbm, w_raw, in_sem.at[4, 0])])
    for some in loads:
        for c in some:
            c.start()

    def loaded(i):
        for c in loads[i]:
            c.wait()

    halo[...] = jnp.zeros_like(halo)
    barrier = pltpu.get_barrier_semaphore()
    for o in range(1, group):
        pl.semaphore_signal(barrier, inc=1, device_id=peer_of(o)[1], device_id_type=MESH)
    for o in range(1, no):
        pl.semaphore_signal(barrier, inc=1, device_id=outer_of(o)[1], device_id_type=MESH)

    vpad[...] = jnp.zeros_like(vpad)
    gpad[...] = jnp.zeros_like(gpad)
    kf[...] = jnp.zeros_like(kf)
    kf[:, 0:cols, width:wide] = jnp.ones((rows, cols, wide - width), BF16)
    qf[...] = jnp.ones_like(qf)
    wpad[...] = jnp.zeros_like(wpad)
    src_f[...] = jnp.zeros_like(src_f)
    stage[...] = jnp.zeros_like(stage)

    def halo_copies(up):
        out = []
        for i, h in enumerate((v_hbm, g_hbm)):
            out.append(pltpu.make_async_remote_copy(
                src_ref=h.at[0, 0] if up else h.at[0, rows - 1],
                dst_ref=halo.at[i, 1 if up else 0],
                send_sem=halo_send.at[i, 1 if up else 0],
                recv_sem=halo_recv.at[i, 1 if up else 0],
                device_id={"band": band - 1 if up else band + 1},
                device_id_type=MESH,
            ))
        return out

    masks = {size: same_head(size) for _, size in groups(wide)}
    ones = {size: masks[size].astype(F32).astype(BF16) for size in masks}

    def spot(index):
        line = index % 16
        tile = index // 16
        return first + tile // per, line, (tile % per) * LANES

    def put(dst, at, size, compact, norm):
        for t in range(size // LANES):
            tile = at // LANES + t
            lane = (tile % per) * LANES
            for h in range(2):
                dst[2 * (tile // per) + h, :, lane : lane + LANES] = compact[
                    16 * h : 16 * h + 16, t * LANES : (t + 1) * LANES]
            slot, line, lane = spot(tile)
            dst[slot, line : line + 1, lane : lane + LANES] = norm[
                :, t * LANES : (t + 1) * LANES]

    def put_forward(at, size, compact, norm):
        for t in range(size // LANES):
            tile = at // LANES + t
            part = slice(t * LANES, (t + 1) * LANES)
            for h in range(4):
                slot, lane = (4 * tile + h) // fper, (4 * tile + h) % fper * LANES
                src_f[slot, :, lane : lane + LANES] = compact[8 * h : 8 * h + 8, part]
            piece = 4 * tiles + tile // 8
            slot, lane, line = piece // fper, piece % fper * LANES, tile % 8
            src_f[slot, line : line + 1, lane : lane + LANES] = norm[:, part]

    def norm_forward(at, size):
        lines = []
        for tile in range(at // LANES, (at + size) // LANES):
            piece = 4 * tiles + tile // 8
            slot, lane, line = piece // fper, piece % fper * LANES, tile % 8
            lines.append(r3_f[slot, line : line + 1, lane : lane + LANES])
        return jnp.concatenate(lines, axis=1) if len(lines) > 1 else lines[0]

    def phase1(way, src, r1):
        out = []
        for o in range(1, group):
            p, dev = peer_of(o)
            c = pltpu.make_async_remote_copy(
                src_ref=src.at[p], dst_ref=r1.at[m], send_sem=s1.at[way, o],
                recv_sem=v1.at[way, m], device_id=dev, device_id_type=MESH)
            c.start()
            out.append(c)
        r1[pl.ds(m, 1)] = src[pl.ds(m, 1)]
        return out

    def wait1(way, src, r1):
        for o in range(1, group):
            p, dev = peer_of(o)
            pltpu.make_async_remote_copy(
                src_ref=src.at[p], dst_ref=r1.at[p], send_sem=s1.at[way, o],
                recv_sem=v1.at[way, p], device_id=dev, device_id_type=MESH).wait_recv()

    def phase2(way, r1, tot, r2):
        total = r1[0].astype(F32)
        for j in range(1, group):
            total = total + r1[j].astype(F32)
        total = total.astype(tot.dtype)
        tot[...] = total
        out = []
        for o in range(1, no):
            zp, dev = outer_of(o)
            c = pltpu.make_async_remote_copy(
                src_ref=tot, dst_ref=r2.at[z], send_sem=s2.at[way, o],
                recv_sem=v2.at[way, z], device_id=dev, device_id_type=MESH)
            c.start()
            out.append(c)
        r2[pl.ds(z, 1)] = total[None]
        return out

    def wait2(way, tot, r2):
        for o in range(1, no):
            zp, dev = outer_of(o)
            pltpu.make_async_remote_copy(
                src_ref=tot, dst_ref=r2.at[zp], send_sem=s2.at[way, o],
                recv_sem=v2.at[way, zp], device_id=dev, device_id_type=MESH).wait_recv()

    def phase3(way, r1, r2, res, r3):
        backward = way == 1
        run = jnp.zeros(tot_f.shape if way == 0 else tot_b.shape, F32)
        whole = run
        for zz in range(no):
            part = r2[zz].astype(F32)
            earlier = (zz > z) if backward else (zz < z)
            run = run + jnp.where(earlier, part, 0.0)
            whole = whole + part
        if backward:
            line = lax.broadcasted_iota(jnp.int32, run.shape, 0)
            tile = lax.broadcasted_iota(jnp.int32, run.shape, 1) // LANES
            extra = ((m - first) * per + tile) * 16 + line >= tiles
        for aa in (range(inner - 1, -1, -1) if backward else range(inner)):
            for bb in range(nb):
                run = run + r1[aa * nb + bb].astype(F32)
            res[aa] = (jnp.where(extra, whole, run) if backward else run).astype(res.dtype)
        out = []
        for o in range(1, group):
            p, dev = peer_of(o)
            c = pltpu.make_async_remote_copy(
                src_ref=res.at[p // nb], dst_ref=r3.at[m], send_sem=s3.at[way, o],
                recv_sem=v3.at[way, m], device_id=dev, device_id_type=MESH)
            c.start()
            out.append(c)
        r3[pl.ds(m, 1)] = res[pl.ds(a, 1)]
        return out

    def wait3(way, res, r3):
        for o in range(1, group):
            p, dev = peer_of(o)
            pltpu.make_async_remote_copy(
                src_ref=res.at[p // nb], dst_ref=r3.at[p], send_sem=s3.at[way, o],
                recv_sem=v3.at[way, p], device_id=dev, device_id_type=MESH).wait_recv()
        if way == 0:
            for tile in range(tiles):
                for h in range(4):
                    slot, lane = (4 * tile + h) // fper, (4 * tile + h) % fper * LANES
                    state[8 * h : 8 * h + 8, tile * LANES : (tile + 1) * LANES] = r3[
                        slot, :, lane : lane + LANES]
            return
        for tile in range(tiles):
            lane = (tile % per) * LANES
            for h in range(2):
                state[16 * h : 16 * h + 16, tile * LANES : (tile + 1) * LANES] = r3[
                    2 * (tile // per) + h, :, lane : lane + LANES].astype(F32)
        extra_s[...] = r3[first:group].astype(F32)

    def norm_of(at, size):
        lines = []
        for t in range(at // LANES, (at + size) // LANES):
            slot, line, lane = spot(t)
            lines.append(extra_s[slot - first, line : line + 1, lane : lane + LANES])
        return jnp.concatenate(lines, axis=1) if len(lines) > 1 else lines[0]

    outs = ((mixed_out, mixed_ref), (qg_out, qg_ref), (kg_out, kg_ref), (vg_out, vg_ref))

    def writes(n):
        held, ref = outs[n]
        return [
            pltpu.make_async_copy(held.at[r], ref.at[0, r], out_sem.at[n, r]) for r in range(rows)
        ]

    def write(n):
        for c in writes(n):
            c.start()

    sent = []
    loaded(0)
    kf[:, 0:cols, 0:width] = feature(k_raw[...].astype(F32)).astype(BF16)
    loaded(1)
    vpad[1 : rows + 1, 0:cols, 0:width] = v_raw[...].astype(F32)
    for at, size in groups(wide):
        kg = kf[:, :, at : at + size].reshape(count, size)
        vg = vpad[1 : rows + 1, :, at : at + size].reshape(count, size).astype(BF16)
        own = compress(mm_at(kg, vg), masks[size])
        norm = jnp.sum(kg.astype(F32), axis=0, keepdims=True)
        put_forward(at, size, own, norm)
    pl.semaphore_wait(barrier, group - 1 + no - 1)
    sent += phase1(0, src_f, r1_f)

    @pl.when(band > 0)
    def _():
        for c in halo_copies(True):
            c.start()

    @pl.when(band < nb - 1)
    def _():
        for c in halo_copies(False):
            c.start()

    loaded(2)
    qf[:, 0:cols, 0:width] = feature(q_raw[...].astype(F32)).astype(BF16)
    loaded(3)
    gpad[1 : rows + 1, 0:cols, 0:width] = g_raw[...].astype(F32)
    loaded(4)
    for i in range(3):
        for j in range(3):
            wpad[3 * i + j : 3 * i + j + 1, 0:width] = w_raw[i, j : j + 1, :]

    def conv(t):
        lanes = pl.ds(pl.multiple_of(t * LANES, LANES), LANES)
        vb = vpad[:, :, lanes]
        gb = gpad[:, :, lanes]
        vs = (pltpu.roll(vb, 1, 1), vb, pltpu.roll(vb, COLS - 1, 1))
        gs = (pltpu.roll(gb, 1, 1), gb, pltpu.roll(gb, COLS - 1, 1))
        own = gb[1 : rows + 1]
        lo = jnp.zeros((rows, COLS, LANES), F32)
        vl = lo
        for i in range(3):
            for j in range(3):
                w = wpad[3 * i + j : 3 * i + j + 1, lanes].reshape(1, 1, LANES)
                near = vs[j][i : i + rows]
                lo = lo + w * near
                vl = vl + w * gs[2 - j][2 - i : 2 - i + rows]
                term = jnp.sum(jnp.sum(own * near, axis=0), axis=0, keepdims=True)
                kterm[3 * i + j : 3 * i + j + 1, lanes] = term
        loc[:, :, lanes] = lo
        vloc[:, :, lanes] = vl

    half = (tiles + 1) // 2
    wait1(0, src_f, r1_f)
    sent += phase2(0, r1_f, tot_f, r2_f)

    @pl.when(band > 0)
    def _():
        for c in halo_copies(False):
            c.wait_recv()

    @pl.when(band < nb - 1)
    def _():
        for c in halo_copies(True):
            c.wait_recv()

    for i, pad in enumerate((vpad, gpad)):
        pad[0, 0:cols, 0:width] = halo[i, 0].astype(F32)
        pad[rows + 1, 0:cols, 0:width] = halo[i, 1].astype(F32)
    pl.loop(0, half)(conv)
    wait2(0, tot_f, r2_f)
    sent += phase3(0, r1_f, r2_f, res_f, r3_f)
    pl.loop(half, tiles)(conv)
    for r in range(9):
        for t in range(tiles):
            slot, line, lane = spot(tiles * (r + 1) + t)
            stage[slot, line : line + 1, lane : lane + LANES] = kterm[
                r : r + 1, t * LANES : (t + 1) * LANES]
    wait3(0, res_f, r3_f)
    blocks = []
    for at, size in groups(wide):
        mask, one = masks[size], ones[size]
        high, low = expand(state[:, at : at + size], mask)
        norm = norm_forward(at, size)
        blocks.append((high, low, norm))
        qg = qf[:, :, at : at + size].reshape(count, size)
        gg = gpad[1 : rows + 1, :, at : at + size].reshape(count, size)
        dh, dl = parts_of(qg.astype(F32) * norm)
        den = mm(dh, one) + mm(dl, one)
        num = mm(qg, high) + mm(qg, low)
        rden = 1.0 / den
        attn = num * rden
        th, tl = parts_of(gg * attn)
        dgw = -(mm(th, one) + mm(tl, one)) * rden
        sh, sl = parts_of(gg * rden)
        own = compress(mm_at(qg, sh) + mm_at(qg, sl), mask)
        put(stage, at, size, own, jnp.sum(qg.astype(F32) * dgw, axis=0, keepdims=True))
        attn_s[:, at : at + size] = attn
        rden_s[:, at : at + size] = rden
        dgw_s[:, at : at + size] = dgw
    src_b[...] = stage[...].astype(BF16)
    sent += phase1(1, src_b, r1_b)
    mixed = (attn_s[...].reshape(rows, COLS, wide) + loc[...]).astype(BF16)
    mixed_out[...] = mixed[:, 0:cols, 0:width]
    write(0)
    wait1(1, src_b, r1_b)
    sent += phase2(1, r1_b, tot_b, r2_b)
    for (at, size), (high, low, norm) in zip(groups(wide), blocks):
        gg = gpad[1 : rows + 1, :, at : at + size].reshape(count, size)
        sh, sl = parts_of(gg * rden_s[:, at : at + size])
        back = mm_bt(sh, high) + mm_bt(sh, low) + mm_bt(sl, high)
        attn_s[:, at : at + size] = back + dgw_s[:, at : at + size] * norm
    grad = attn_s[...].reshape(rows, COLS, wide)[:, 0:cols, 0:width]
    qg_out[...] = (grad * slope(q_raw[...].astype(F32))).astype(BF16)
    write(1)
    wait2(1, tot_b, r2_b)
    sent += phase3(1, r1_b, r2_b, res_b, r3_b)
    steep = slope(k_raw[...].astype(F32))
    dgw_s[...] = jnp.ones_like(dgw_s)
    for r in range(rows):
        dgw_s[r * COLS : r * COLS + cols, 0:width] = steep[r]
    wait3(1, res_b, r3_b)

    def send_out(n, held, made):
        held[...] = made[...].reshape(rows, COLS, wide)[:, 0:cols, 0:width].astype(BF16)
        write(n)

    later = []
    for at, size in groups(wide):
        high, low = expand(state[:, at : at + size], masks[size])
        norm = norm_of(at, size)
        later.append((high, low))
        vg = vpad[1 : rows + 1, :, at : at + size].reshape(count, size).astype(BF16)
        back = mm_bt(vg, high) + mm_bt(vg, low) + norm
        attn_s[:, at : at + size] = back * dgw_s[:, at : at + size]
    send_out(2, kg_out, attn_s)
    for (at, size), (high, low) in zip(groups(wide), later):
        kg = kf[:, :, at : at + size].reshape(count, size)
        rden_s[:, at : at + size] = mm(kg, high) + mm(kg, low) + vloc[
            :, :, at : at + size].reshape(count, size)
    send_out(3, vg_out, rden_s)
    tokens = lax.axis_size("tm") * nb * rows * cols
    for r in range(9):
        for t in range(tiles):
            slot, line, lane = spot(tiles * (r + 1) + t)
            size = min(LANES, width - t * LANES)
            term = extra_s[slot - first, line : line + 1, lane : lane + size]
            wg_out[r // 3, r % 3 : r % 3 + 1, t * LANES : t * LANES + size] = term * (
                1.0 / math.sqrt(tokens))

    pltpu.make_async_copy(wg_out, wg_ref, out_sem.at[4, 0]).start()
    for n in range(4):
        for c in writes(n):
            c.wait()
    pltpu.make_async_copy(wg_out, wg_ref, out_sem.at[4, 0]).wait()
    for c in sent:
        c.wait_send()

    @pl.when(band > 0)
    def _():
        for c in halo_copies(True):
            c.wait_send()

    @pl.when(band < nb - 1)
    def _():
        for c in halo_copies(False):
            c.wait_send()


def shards(query_input, key_input, value_input, cotangent, local_kernel_weight):
    _, rows, cols, width = query_input.shape
    wide = -(-width // LANES) * LANES
    frames, nb = lax.axis_size("tm"), lax.axis_size("band")
    inner = 4
    no = frames // inner
    group = nb * inner
    tiles = wide // LANES
    per = -(-tiles // (group // 2))
    first = 2 * -(-tiles // per)
    lanes = per * LANES
    fper = -(-(4 * tiles + -(-tiles // 8)) // group)
    count = rows * COLS
    cfg = (rows, cols, width, wide, nb, no, inner, per, first, fper)
    raw = pltpu.VMEM((rows, cols, width), BF16)

    def buffers(r, lanes, kind):
        return [
            pltpu.VMEM((n, r, lanes) if n else (r, lanes), kind)
            for n in (group, group, 0, no, inner, group)
        ]

    tok = jax.ShapeDtypeStruct(query_input.shape, BF16)
    dma = pltpu.SemaphoreType.DMA
    made = pl.pallas_call(
        functools.partial(kernel, cfg),
        out_shape=(tok, tok, tok, tok, jax.ShapeDtypeStruct(local_kernel_weight.shape, F32)),
        in_specs=[pl.BlockSpec(memory_space=pltpu.HBM)] * 5,
        out_specs=[pl.BlockSpec(memory_space=pl.ANY)] * 5,
        scratch_shapes=[
            raw, raw, raw, raw, raw, raw, raw, raw,
            pltpu.VMEM(local_kernel_weight.shape, F32), dma((5, rows)),
            pltpu.VMEM((2, 2, cols, width), BF16),
            pltpu.VMEM((rows + 2, COLS, wide), F32), pltpu.VMEM((rows + 2, COLS, wide), F32),
            pltpu.VMEM((rows, COLS, wide), BF16), pltpu.VMEM((rows, COLS, wide), BF16),
            pltpu.VMEM((16, wide), F32),
            pltpu.VMEM((rows, COLS, wide), F32), pltpu.VMEM((rows, COLS, wide), F32),
            pltpu.VMEM((16, wide), F32),
            pltpu.VMEM((count, wide), F32), pltpu.VMEM((count, wide), F32),
            pltpu.VMEM((count, wide), F32),
            pltpu.VMEM((HEAD_DIM, wide), F32),
            pltpu.VMEM((group, 16, lanes), F32), pltpu.VMEM((group - first, 16, lanes), F32),
            pltpu.VMEM(local_kernel_weight.shape, F32),
            *buffers(8, fper * LANES, F32), *buffers(16, lanes, BF16),
            dma((5, rows)), dma((2, 2)), dma((2, 2)),
            dma((2, group)), dma((2, group)), dma((2, no)), dma((2, no)),
            dma((2, group)), dma((2, group)),
        ],
        compiler_params=pltpu.CompilerParams(
            collective_id=0, has_side_effects=True, vmem_limit_bytes=62 * 1024 * 1024
        ),
        cost_estimate=pl.CostEstimate(flops=10**9, bytes_accessed=3 * 10**6, transcendentals=0),
        name="block_causal",
    )(query_input, key_input, value_input, cotangent, local_kernel_weight)
    return pl.pallas_call(
        hand_over,
        out_shape=tuple(jax.ShapeDtypeStruct(x.shape, x.dtype) for x in made),
        in_specs=[pl.BlockSpec(memory_space=pl.ANY)] * 5,
        out_specs=[pl.BlockSpec(memory_space=pltpu.HBM)] * 5,
        scratch_shapes=[pltpu.VMEM(x.shape, x.dtype) for x in made]
        + [dma((5,)), dma((5,))],
        compiler_params=pltpu.CompilerParams(vmem_limit_bytes=62 * 1024 * 1024),
        name="hand_over",
    )(*made)


def hand_over(*refs):
    pieces = []
    for i in range(5):
        src, dst, held = refs[i], refs[5 + i], refs[10 + i]
        pieces.append((
            pltpu.make_async_copy(src, held, refs[15].at[i]),
            pltpu.make_async_copy(held, dst, refs[16].at[i]),
        ))
    for load, _ in pieces:
        load.start()
    for load, store in pieces:
        load.wait()
        store.start()
    for _, store in pieces:
        store.wait()


def solution(mesh):
    token = P("tm", "band", None, None)
    return jax.shard_map(
        shards,
        mesh=mesh,
        in_specs=(token,) * 4 + (P(),),
        out_specs=(token,) * 4 + (P(),),
        check_vma=False,
    )
```

```python
import functools
import math

import jax
import jax.numpy as jnp
from jax import lax
from jax.experimental import pallas as pl
from jax.experimental.pallas import tpu as pltpu
from jax.sharding import PartitionSpec as P

HEAD_DIM = 32
LANES = 128
COLS = 32
MESH = pl.DeviceIdType.MESH
F32 = jnp.float32
BF16 = jnp.bfloat16


def groups(wide):
    out, at = [], 0
    while at < wide:
        size = min(256, wide - at)
        out.append((at, size))
        at += size
    return out


def feature(x):
    return jnp.where(x > 0, x + 1.0, jnp.exp(jnp.minimum(x, 0.0)))


def slope(x):
    return jnp.where(x > 0, 1.0, jnp.exp(jnp.minimum(x, 0.0)))


def parts_of(x):
    high = x.astype(BF16)
    return high, (x - high.astype(F32)).astype(BF16)


def mm(a, b):
    return lax.dot_general(a, b, (((1,), (0,)), ((), ())), preferred_element_type=F32)


def mm_bt(a, b):
    return lax.dot_general(a, b, (((1,), (1,)), ((), ())), preferred_element_type=F32)


def mm_at(a, b):
    return lax.dot_general(a, b, (((0,), (0,)), ((), ())), preferred_element_type=F32)


def same_head(size):
    row = lax.broadcasted_iota(jnp.int32, (size, size), 0) // HEAD_DIM
    lane = lax.broadcasted_iota(jnp.int32, (size, size), 1) // HEAD_DIM
    return row == lane


def compress(full, mask):
    size = full.shape[0]
    kept = jnp.where(mask, full, 0.0)
    total = kept[0:HEAD_DIM]
    for h in range(1, size // HEAD_DIM):
        total = total + kept[h * HEAD_DIM : (h + 1) * HEAD_DIM]
    return total


def expand(compact, mask):
    size = compact.shape[1]
    tiled = jnp.concatenate([compact] * (size // HEAD_DIM), axis=0)
    return parts_of(jnp.where(mask, tiled, 0.0))


def kernel(cfg, q_hbm, k_hbm, v_hbm, g_hbm, w_hbm, mixed_ref, qg_ref, kg_ref, vg_ref, wg_ref,
           q_raw, k_raw, v_raw, g_raw, mixed_out, qg_out, kg_out, vg_out, wg_out, out_sem, halo, vpad, gpad, qf, kf, wpad, loc, vloc, kterm,
           attn_s, rden_s, dgw_s, state, stage, extra_s, w_raw, src_f, r1_f, tot_f, r2_f, res_f, r3_f,
           src_b, r1_b, tot_b, r2_b, res_b, r3_b,
           in_sem, halo_send, halo_recv, s1, v1, s2, v2, s3, v3):
    rows, cols, width, wide, nb, no, inner, per, first, fper = cfg
    group = nb * inner
    count = rows * COLS
    tm = lax.axis_index("tm")
    band = lax.axis_index("band")
    z = tm // inner
    tiles = wide // LANES
    a = tm % inner
    m = a * nb + band

    def placed(p):
        frame = lax.div(p, nb)
        return p, frame, {"tm": z * inner + frame, "band": lax.rem(p, nb)}

    peers = [None] + [placed(lax.rem(m + o, group)) for o in range(1, group)]
    outers = [lax.rem(z + o, no) for o in range(no)]

    def peer_of(o):
        return peers[o][0], peers[o][2]

    def outer_of(o):
        return outers[o], {"tm": outers[o] * inner + a, "band": band}

    loads = [
        pltpu.make_async_copy(h.at[0], d, in_sem.at[i])
        for i, (h, d) in enumerate(((k_hbm, k_raw), (v_hbm, v_raw), (q_hbm, q_raw), (g_hbm, g_raw)))
    ]
    loads.append(pltpu.make_async_copy(w_hbm, w_raw, in_sem.at[4]))
    for c in loads[:2]:
        c.start()

    def loaded(i):
        loads[i].wait()

    halo[...] = jnp.zeros_like(halo)
    barrier = pltpu.get_barrier_semaphore()
    for o in range(1, group):
        pl.semaphore_signal(barrier, inc=1, device_id=peer_of(o)[1], device_id_type=MESH)
    for o in range(1, no):
        pl.semaphore_signal(barrier, inc=1, device_id=outer_of(o)[1], device_id_type=MESH)

    for c in loads[2:]:
        c.start()
    vpad[...] = jnp.zeros_like(vpad)
    gpad[...] = jnp.zeros_like(gpad)
    kf[...] = jnp.zeros_like(kf)
    kf[:, 0:cols, width:wide] = jnp.ones((rows, cols, wide - width), BF16)
    qf[...] = jnp.ones_like(qf)
    wpad[...] = jnp.zeros_like(wpad)
    src_f[...] = jnp.zeros_like(src_f)
    stage[...] = jnp.zeros_like(stage)

    def halo_copies(up):
        out = []
        for i, h in enumerate((v_hbm, g_hbm)):
            out.append(pltpu.make_async_remote_copy(
                src_ref=h.at[0, 0] if up else h.at[0, rows - 1],
                dst_ref=halo.at[i, 1 if up else 0],
                send_sem=halo_send.at[i, 1 if up else 0],
                recv_sem=halo_recv.at[i, 1 if up else 0],
                device_id={"band": band - 1 if up else band + 1},
                device_id_type=MESH,
            ))
        return out

    masks = {size: same_head(size) for _, size in groups(wide)}
    ones = {size: masks[size].astype(F32).astype(BF16) for size in masks}

    def spot(index):
        line = index % 16
        tile = index // 16
        return first + tile // per, line, (tile % per) * LANES

    def put(dst, at, size, compact, norm):
        for t in range(size // LANES):
            tile = at // LANES + t
            lane = (tile % per) * LANES
            for h in range(2):
                dst[2 * (tile // per) + h, :, lane : lane + LANES] = compact[
                    16 * h : 16 * h + 16, t * LANES : (t + 1) * LANES]
            slot, line, lane = spot(tile)
            dst[slot, line : line + 1, lane : lane + LANES] = norm[
                :, t * LANES : (t + 1) * LANES]

    def put_forward(at, size, compact, norm):
        for t in range(size // LANES):
            tile = at // LANES + t
            part = slice(t * LANES, (t + 1) * LANES)
            for h in range(4):
                slot, lane = (4 * tile + h) // fper, (4 * tile + h) % fper * LANES
                src_f[slot, :, lane : lane + LANES] = compact[8 * h : 8 * h + 8, part]
            piece = 4 * tiles + tile // 8
            slot, lane, line = piece // fper, piece % fper * LANES, tile % 8
            src_f[slot, line : line + 1, lane : lane + LANES] = norm[:, part]

    def norm_forward(at, size):
        lines = []
        for tile in range(at // LANES, (at + size) // LANES):
            piece = 4 * tiles + tile // 8
            slot, lane, line = piece // fper, piece % fper * LANES, tile % 8
            lines.append(r3_f[slot, line : line + 1, lane : lane + LANES])
        return jnp.concatenate(lines, axis=1) if len(lines) > 1 else lines[0]

    def phase1(way, src, r1):
        out = []
        for o in range(1, group):
            p, dev = peer_of(o)
            c = pltpu.make_async_remote_copy(
                src_ref=src.at[p], dst_ref=r1.at[m], send_sem=s1.at[way, o],
                recv_sem=v1.at[way, m], device_id=dev, device_id_type=MESH)
            c.start()
            out.append(c)
        r1[pl.ds(m, 1)] = src[pl.ds(m, 1)]
        return out

    def wait1(way, src, r1):
        for o in range(1, group):
            p, dev = peer_of(o)
            pltpu.make_async_remote_copy(
                src_ref=src.at[p], dst_ref=r1.at[p], send_sem=s1.at[way, o],
                recv_sem=v1.at[way, p], device_id=dev, device_id_type=MESH).wait_recv()

    def phase2(way, r1, tot, r2):
        total = r1[0].astype(F32)
        for j in range(1, group):
            total = total + r1[j].astype(F32)
        total = total.astype(tot.dtype)
        tot[...] = total
        out = []
        for o in range(1, no):
            zp, dev = outer_of(o)
            c = pltpu.make_async_remote_copy(
                src_ref=tot, dst_ref=r2.at[z], send_sem=s2.at[way, o],
                recv_sem=v2.at[way, z], device_id=dev, device_id_type=MESH)
            c.start()
            out.append(c)
        r2[pl.ds(z, 1)] = total[None]
        return out

    def wait2(way, tot, r2):
        for o in range(1, no):
            zp, dev = outer_of(o)
            pltpu.make_async_remote_copy(
                src_ref=tot, dst_ref=r2.at[zp], send_sem=s2.at[way, o],
                recv_sem=v2.at[way, zp], device_id=dev, device_id_type=MESH).wait_recv()

    def phase3(way, r1, r2, res, r3):
        backward = way == 1
        run = jnp.zeros(tot_f.shape if way == 0 else tot_b.shape, F32)
        whole = run
        for zz in range(no):
            part = r2[zz].astype(F32)
            earlier = (zz > z) if backward else (zz < z)
            run = run + jnp.where(earlier, part, 0.0)
            whole = whole + part
        if backward:
            line = lax.broadcasted_iota(jnp.int32, run.shape, 0)
            tile = lax.broadcasted_iota(jnp.int32, run.shape, 1) // LANES
            extra = ((m - first) * per + tile) * 16 + line >= tiles
        for aa in (range(inner - 1, -1, -1) if backward else range(inner)):
            for bb in range(nb):
                run = run + r1[aa * nb + bb].astype(F32)
            res[aa] = (jnp.where(extra, whole, run) if backward else run).astype(res.dtype)
        out = []
        for o in range(1, group):
            p, dev = peer_of(o)
            c = pltpu.make_async_remote_copy(
                src_ref=res.at[peers[o][1]], dst_ref=r3.at[m], send_sem=s3.at[way, o],
                recv_sem=v3.at[way, m], device_id=dev, device_id_type=MESH)
            c.start()
            out.append(c)
        r3[pl.ds(m, 1)] = res[pl.ds(a, 1)]
        return out

    def wait3(way, res, r3):
        for o in range(1, group):
            p, dev = peer_of(o)
            pltpu.make_async_remote_copy(
                src_ref=res.at[peers[o][1]], dst_ref=r3.at[p], send_sem=s3.at[way, o],
                recv_sem=v3.at[way, p], device_id=dev, device_id_type=MESH).wait_recv()
        if way == 0:
            for tile in range(tiles):
                for h in range(4):
                    slot, lane = (4 * tile + h) // fper, (4 * tile + h) % fper * LANES
                    state[8 * h : 8 * h + 8, tile * LANES : (tile + 1) * LANES] = r3[
                        slot, :, lane : lane + LANES]
            return
        for tile in range(tiles):
            lane = (tile % per) * LANES
            for h in range(2):
                state[16 * h : 16 * h + 16, tile * LANES : (tile + 1) * LANES] = r3[
                    2 * (tile // per) + h, :, lane : lane + LANES].astype(F32)
        extra_s[...] = r3[first:group].astype(F32)

    def norm_of(at, size):
        lines = []
        for t in range(at // LANES, (at + size) // LANES):
            slot, line, lane = spot(t)
            lines.append(extra_s[slot - first, line : line + 1, lane : lane + LANES])
        return jnp.concatenate(lines, axis=1) if len(lines) > 1 else lines[0]

    outs = ((mixed_out, mixed_ref), (qg_out, qg_ref), (kg_out, kg_ref), (vg_out, vg_ref))

    def writes(n):
        held, ref = outs[n]
        return pltpu.make_async_copy(held, ref.at[0], out_sem.at[n])

    def write(n):
        writes(n).start()

    sent = []
    loaded(0)
    kf[:, 0:cols, 0:width] = feature(k_raw[...].astype(F32)).astype(BF16)
    loaded(1)
    vpad[1 : rows + 1, 0:cols, 0:width] = v_raw[...].astype(F32)
    for at, size in groups(wide):
        kg = kf[:, :, at : at + size].reshape(count, size)
        vg = vpad[1 : rows + 1, :, at : at + size].reshape(count, size).astype(BF16)
        own = compress(mm_at(kg, vg), masks[size])
        norm = jnp.sum(kg.astype(F32), axis=0, keepdims=True)
        put_forward(at, size, own, norm)
    pl.semaphore_wait(barrier, group - 1 + no - 1)
    sent += phase1(0, src_f, r1_f)

    @pl.when(band > 0)
    def _():
        for c in halo_copies(True):
            c.start()

    @pl.when(band < nb - 1)
    def _():
        for c in halo_copies(False):
            c.start()

    loaded(2)
    qf[:, 0:cols, 0:width] = feature(q_raw[...].astype(F32)).astype(BF16)
    loaded(3)
    gpad[1 : rows + 1, 0:cols, 0:width] = g_raw[...].astype(F32)
    loaded(4)
    for i in range(3):
        for j in range(3):
            wpad[3 * i + j : 3 * i + j + 1, 0:width] = w_raw[i, j : j + 1, :]

    def conv(t):
        lanes = pl.ds(pl.multiple_of(t * LANES, LANES), LANES)
        vb = vpad[:, :, lanes]
        gb = gpad[:, :, lanes]
        vs = (pltpu.roll(vb, 1, 1), vb, pltpu.roll(vb, COLS - 1, 1))
        gs = (pltpu.roll(gb, 1, 1), gb, pltpu.roll(gb, COLS - 1, 1))
        own = gb[1 : rows + 1]
        lo = jnp.zeros((rows, COLS, LANES), F32)
        vl = lo
        for i in range(3):
            for j in range(3):
                w = wpad[3 * i + j : 3 * i + j + 1, lanes].reshape(1, 1, LANES)
                near = vs[j][i : i + rows]
                lo = lo + w * near
                vl = vl + w * gs[2 - j][2 - i : 2 - i + rows]
                term = jnp.sum(jnp.sum(own * near, axis=0), axis=0, keepdims=True)
                kterm[3 * i + j : 3 * i + j + 1, lanes] = term
        loc[:, :, lanes] = lo
        vloc[:, :, lanes] = vl

    half = (tiles + 1) // 2
    wait1(0, src_f, r1_f)
    sent += phase2(0, r1_f, tot_f, r2_f)

    @pl.when(band > 0)
    def _():
        for c in halo_copies(False):
            c.wait_recv()

    @pl.when(band < nb - 1)
    def _():
        for c in halo_copies(True):
            c.wait_recv()

    for i, pad in enumerate((vpad, gpad)):
        pad[0, 0:cols, 0:width] = halo[i, 0].astype(F32)
        pad[rows + 1, 0:cols, 0:width] = halo[i, 1].astype(F32)
    pl.loop(0, half)(conv)
    wait2(0, tot_f, r2_f)
    sent += phase3(0, r1_f, r2_f, res_f, r3_f)
    pl.loop(half, tiles)(conv)
    for r in range(9):
        for t in range(tiles):
            slot, line, lane = spot(tiles * (r + 1) + t)
            stage[slot, line : line + 1, lane : lane + LANES] = kterm[
                r : r + 1, t * LANES : (t + 1) * LANES]
    wait3(0, res_f, r3_f)
    blocks = []
    for at, size in groups(wide):
        mask, one = masks[size], ones[size]
        high, low = expand(state[:, at : at + size], mask)
        norm = norm_forward(at, size)
        blocks.append((high, low, norm))
        qg = qf[:, :, at : at + size].reshape(count, size)
        gg = gpad[1 : rows + 1, :, at : at + size].reshape(count, size)
        dh, dl = parts_of(qg.astype(F32) * norm)
        den = mm(dh, one) + mm(dl, one)
        num = mm(qg, high) + mm(qg, low)
        rden = 1.0 / den
        attn = num * rden
        th, tl = parts_of(gg * attn)
        dgw = -(mm(th, one) + mm(tl, one)) * rden
        sh, sl = parts_of(gg * rden)
        own = compress(mm_at(qg, sh) + mm_at(qg, sl), mask)
        put(stage, at, size, own, jnp.sum(qg.astype(F32) * dgw, axis=0, keepdims=True))
        attn_s[:, at : at + size] = attn
        rden_s[:, at : at + size] = rden
        dgw_s[:, at : at + size] = dgw
    src_b[...] = stage[...].astype(BF16)
    sent += phase1(1, src_b, r1_b)
    mixed = (attn_s[...].reshape(rows, COLS, wide) + loc[...]).astype(BF16)
    mixed_out[...] = mixed[:, 0:cols, 0:width]
    write(0)
    wait1(1, src_b, r1_b)
    sent += phase2(1, r1_b, tot_b, r2_b)
    for (at, size), (high, low, norm) in zip(groups(wide), blocks):
        gg = gpad[1 : rows + 1, :, at : at + size].reshape(count, size)
        sh, sl = parts_of(gg * rden_s[:, at : at + size])
        back = mm_bt(sh, high) + mm_bt(sh, low) + mm_bt(sl, high)
        attn_s[:, at : at + size] = back + dgw_s[:, at : at + size] * norm
    grad = attn_s[...].reshape(rows, COLS, wide)[:, 0:cols, 0:width]
    qg_out[...] = (grad * slope(q_raw[...].astype(F32))).astype(BF16)
    write(1)
    wait2(1, tot_b, r2_b)
    sent += phase3(1, r1_b, r2_b, res_b, r3_b)
    for c in sent[: -(group - 1)]:
        c.wait_send()

    @pl.when(band > 0)
    def _():
        for c in halo_copies(True):
            c.wait_send()

    @pl.when(band < nb - 1)
    def _():
        for c in halo_copies(False):
            c.wait_send()

    steep = slope(k_raw[...].astype(F32))
    dgw_s[...] = jnp.ones_like(dgw_s)
    for r in range(rows):
        dgw_s[r * COLS : r * COLS + cols, 0:width] = steep[r]
    wait3(1, res_b, r3_b)

    def send_out(n, held, made):
        held[...] = made[...].reshape(rows, COLS, wide)[:, 0:cols, 0:width].astype(BF16)
        write(n)

    later = []
    for at, size in groups(wide):
        high, low = expand(state[:, at : at + size], masks[size])
        norm = norm_of(at, size)
        later.append((high, low))
        vg = vpad[1 : rows + 1, :, at : at + size].reshape(count, size).astype(BF16)
        back = mm_bt(vg, high) + mm_bt(vg, low) + norm
        attn_s[:, at : at + size] = back * dgw_s[:, at : at + size]
    send_out(2, kg_out, attn_s)
    for (at, size), (high, low) in zip(groups(wide), later):
        kg = kf[:, :, at : at + size].reshape(count, size)
        rden_s[:, at : at + size] = mm(kg, high) + mm(kg, low) + vloc[
            :, :, at : at + size].reshape(count, size)
    send_out(3, vg_out, rden_s)
    tokens = lax.axis_size("tm") * nb * rows * cols
    for r in range(9):
        for t in range(tiles):
            slot, line, lane = spot(tiles * (r + 1) + t)
            size = min(LANES, width - t * LANES)
            term = extra_s[slot - first, line : line + 1, lane : lane + size]
            wg_out[r // 3, r % 3 : r % 3 + 1, t * LANES : t * LANES + size] = term * (
                1.0 / math.sqrt(tokens))

    pltpu.make_async_copy(wg_out, wg_ref, out_sem.at[4]).start()
    for n in range(4):
        writes(n).wait()
    pltpu.make_async_copy(wg_out, wg_ref, out_sem.at[4]).wait()
    for c in sent[-(group - 1) :]:
        c.wait_send()


def shards(query_input, key_input, value_input, cotangent, local_kernel_weight):
    _, rows, cols, width = query_input.shape
    wide = -(-width // LANES) * LANES
    frames, nb = lax.axis_size("tm"), lax.axis_size("band")
    inner = 4
    no = frames // inner
    group = nb * inner
    tiles = wide // LANES
    per = -(-tiles // (group // 2))
    first = 2 * -(-tiles // per)
    lanes = per * LANES
    fper = -(-(4 * tiles + -(-tiles // 8)) // group)
    count = rows * COLS
    cfg = (rows, cols, width, wide, nb, no, inner, per, first, fper)
    raw = pltpu.VMEM((rows, cols, width), BF16)

    def buffers(r, lanes, kind):
        return [
            pltpu.VMEM((n, r, lanes) if n else (r, lanes), kind)
            for n in (group, group, 0, no, inner, group)
        ]

    tok = jax.ShapeDtypeStruct(query_input.shape, BF16)
    dma = pltpu.SemaphoreType.DMA
    made = pl.pallas_call(
        functools.partial(kernel, cfg),
        out_shape=(tok, tok, tok, tok, jax.ShapeDtypeStruct(local_kernel_weight.shape, F32)),
        in_specs=[pl.BlockSpec(memory_space=pltpu.HBM)] * 5,
        out_specs=[pl.BlockSpec(memory_space=pl.ANY)] * 5,
        scratch_shapes=[
            raw, raw, raw, raw, raw, raw, raw, raw,
            pltpu.VMEM(local_kernel_weight.shape, F32), dma((5,)),
            pltpu.VMEM((2, 2, cols, width), BF16),
            pltpu.VMEM((rows + 2, COLS, wide), F32), pltpu.VMEM((rows + 2, COLS, wide), F32),
            pltpu.VMEM((rows, COLS, wide), BF16), pltpu.VMEM((rows, COLS, wide), BF16),
            pltpu.VMEM((16, wide), F32),
            pltpu.VMEM((rows, COLS, wide), F32), pltpu.VMEM((rows, COLS, wide), F32),
            pltpu.VMEM((16, wide), F32),
            pltpu.VMEM((count, wide), F32), pltpu.VMEM((count, wide), F32),
            pltpu.VMEM((count, wide), F32),
            pltpu.VMEM((HEAD_DIM, wide), F32),
            pltpu.VMEM((group, 16, lanes), F32), pltpu.VMEM((group - first, 16, lanes), F32),
            pltpu.VMEM(local_kernel_weight.shape, F32),
            *buffers(8, fper * LANES, F32), *buffers(16, lanes, BF16),
            dma((5,)), dma((2, 2)), dma((2, 2)),
            dma((2, group)), dma((2, group)), dma((2, no)), dma((2, no)),
            dma((2, group)), dma((2, group)),
        ],
        compiler_params=pltpu.CompilerParams(
            collective_id=0, has_side_effects=True, vmem_limit_bytes=62 * 1024 * 1024
        ),
        cost_estimate=pl.CostEstimate(flops=10**9, bytes_accessed=3 * 10**6, transcendentals=0),
        name="block_causal",
    )(query_input, key_input, value_input, cotangent, local_kernel_weight)
    return pl.pallas_call(
        hand_over,
        out_shape=tuple(jax.ShapeDtypeStruct(x.shape, x.dtype) for x in made),
        in_specs=[pl.BlockSpec(memory_space=pl.ANY)] * 5,
        out_specs=[pl.BlockSpec(memory_space=pltpu.HBM)] * 5,
        scratch_shapes=[pltpu.VMEM(x.shape, x.dtype) for x in made]
        + [dma((5,)), dma((5,))],
        compiler_params=pltpu.CompilerParams(vmem_limit_bytes=62 * 1024 * 1024),
        name="hand_over",
    )(*made)


def hand_over(*refs):
    pieces = []
    for i in range(5):
        src, dst, held = refs[i], refs[5 + i], refs[10 + i]
        pieces.append((
            pltpu.make_async_copy(src, held, refs[15].at[i]),
            pltpu.make_async_copy(held, dst, refs[16].at[i]),
        ))
    for load, _ in pieces:
        load.start()
    for load, store in pieces:
        load.wait()
        store.start()
    for _, store in pieces:
        store.wait()


def solution(mesh):
    token = P("tm", "band", None, None)
    return jax.shard_map(
        shards,
        mesh=mesh,
        in_specs=(token,) * 4 + (P(),),
        out_specs=(token,) * 4 + (P(),),
        check_vma=False,
    )
```

```python
import functools
import math

import jax
import jax.numpy as jnp
from jax import lax
from jax.experimental import pallas as pl
from jax.experimental.pallas import tpu as pltpu
from jax.sharding import PartitionSpec as P

HEAD_DIM = 32
LANES = 128
COLS = 32
MESH = pl.DeviceIdType.MESH
F32 = jnp.float32
BF16 = jnp.bfloat16


def groups(wide):
    out, at = [], 0
    while at < wide:
        size = min(256, wide - at)
        out.append((at, size))
        at += size
    return out


def feature(x):
    return jnp.where(x > 0, x + 1.0, jnp.exp(jnp.minimum(x, 0.0)))


def slope(x):
    return jnp.where(x > 0, 1.0, jnp.exp(jnp.minimum(x, 0.0)))


def parts_of(x):
    high = x.astype(BF16)
    return high, (x - high.astype(F32)).astype(BF16)


def mm(a, b):
    return lax.dot_general(a, b, (((1,), (0,)), ((), ())), preferred_element_type=F32)


def mm_bt(a, b):
    return lax.dot_general(a, b, (((1,), (1,)), ((), ())), preferred_element_type=F32)


def mm_at(a, b):
    return lax.dot_general(a, b, (((0,), (0,)), ((), ())), preferred_element_type=F32)


def same_head(size):
    row = lax.broadcasted_iota(jnp.int32, (size, size), 0) // HEAD_DIM
    lane = lax.broadcasted_iota(jnp.int32, (size, size), 1) // HEAD_DIM
    return row == lane


def compress(full, mask):
    size = full.shape[0]
    kept = jnp.where(mask, full, 0.0)
    total = kept[0:HEAD_DIM]
    for h in range(1, size // HEAD_DIM):
        total = total + kept[h * HEAD_DIM : (h + 1) * HEAD_DIM]
    return total


def expand(compact, mask):
    size = compact.shape[1]
    tiled = jnp.concatenate([compact] * (size // HEAD_DIM), axis=0)
    return parts_of(jnp.where(mask, tiled, 0.0))


def kernel(cfg, q_hbm, k_hbm, v_hbm, g_hbm, w_hbm, mixed_ref, qg_ref, kg_ref, vg_ref, wg_ref,
           q_raw, k_raw, v_raw, g_raw, mixed_out, qg_out, kg_out, vg_out, wg_out, out_sem, halo, vpad, gpad, qf, kf, wpad, loc, vloc, kterm,
           attn_s, rden_s, dgw_s, state, stage, extra_s, w_raw, src_f, r1_f, tot_f, r2_f, res_f, r3_f,
           src_b, r1_b, tot_b, r2_b, res_b, r3_b,
           in_sem, halo_send, halo_recv, s1, v1, s2, v2, s3, v3):
    rows, cols, width, wide, nb, no, inner, per, first, fper = cfg
    group = nb * inner
    count = rows * COLS
    tm = lax.axis_index("tm")
    band = lax.axis_index("band")
    z = tm // inner
    tiles = wide // LANES
    a = tm % inner
    m = a * nb + band

    def placed(p):
        frame = lax.div(p, nb)
        return p, frame, {"tm": z * inner + frame, "band": lax.rem(p, nb)}

    peers = [None] + [placed(lax.rem(m + o, group)) for o in range(1, group)]
    outers = [lax.rem(z + o, no) for o in range(no)]

    def peer_of(o):
        return peers[o][0], peers[o][2]

    def outer_of(o):
        return outers[o], {"tm": outers[o] * inner + a, "band": band}

    loads = [
        pltpu.make_async_copy(h.at[0], d, in_sem.at[i])
        for i, (h, d) in enumerate(((k_hbm, k_raw), (v_hbm, v_raw), (q_hbm, q_raw), (g_hbm, g_raw)))
    ]
    loads.append(pltpu.make_async_copy(w_hbm, w_raw, in_sem.at[4]))
    for c in loads[:2]:
        c.start()

    def loaded(i):
        loads[i].wait()

    halo[...] = jnp.zeros_like(halo)
    barrier = pltpu.get_barrier_semaphore()
    for o in range(1, group):
        pl.semaphore_signal(barrier, inc=1, device_id=peer_of(o)[1], device_id_type=MESH)
    for o in range(1, no):
        pl.semaphore_signal(barrier, inc=1, device_id=outer_of(o)[1], device_id_type=MESH)

    for c in loads[2:]:
        c.start()
    vpad[...] = jnp.zeros_like(vpad)
    gpad[...] = jnp.zeros_like(gpad)
    kf[...] = jnp.zeros_like(kf)
    kf[:, 0:cols, width:wide] = jnp.ones((rows, cols, wide - width), BF16)
    qf[...] = jnp.ones_like(qf)
    wpad[...] = jnp.zeros_like(wpad)
    src_f[...] = jnp.zeros_like(src_f)
    stage[...] = jnp.zeros_like(stage)

    def halo_copies(up):
        out = []
        for i, h in enumerate((v_hbm, g_hbm)):
            out.append(pltpu.make_async_remote_copy(
                src_ref=h.at[0, 0] if up else h.at[0, rows - 1],
                dst_ref=halo.at[i, 1 if up else 0],
                send_sem=halo_send.at[i, 1 if up else 0],
                recv_sem=halo_recv.at[i, 1 if up else 0],
                device_id={"band": band - 1 if up else band + 1},
                device_id_type=MESH,
            ))
        return out

    masks = {size: same_head(size) for _, size in groups(wide)}
    ones = {size: masks[size].astype(F32).astype(BF16) for size in masks}

    def spot(index):
        line = index % 16
        tile = index // 16
        return first + tile // per, line, (tile % per) * LANES

    def put(dst, at, size, compact, norm):
        for t in range(size // LANES):
            tile = at // LANES + t
            lane = (tile % per) * LANES
            for h in range(2):
                dst[2 * (tile // per) + h, :, lane : lane + LANES] = compact[
                    16 * h : 16 * h + 16, t * LANES : (t + 1) * LANES]
            slot, line, lane = spot(tile)
            dst[slot, line : line + 1, lane : lane + LANES] = norm[
                :, t * LANES : (t + 1) * LANES]

    def put_forward(at, size, compact, norm):
        for t in range(size // LANES):
            tile = at // LANES + t
            part = slice(t * LANES, (t + 1) * LANES)
            for h in range(4):
                slot, lane = (4 * tile + h) // fper, (4 * tile + h) % fper * LANES
                src_f[slot, :, lane : lane + LANES] = compact[8 * h : 8 * h + 8, part]
            piece = 4 * tiles + tile // 8
            slot, lane, line = piece // fper, piece % fper * LANES, tile % 8
            src_f[slot, line : line + 1, lane : lane + LANES] = norm[:, part]

    def norm_forward(at, size):
        lines = []
        for tile in range(at // LANES, (at + size) // LANES):
            piece = 4 * tiles + tile // 8
            slot, lane, line = piece // fper, piece % fper * LANES, tile % 8
            lines.append(r3_f[slot, line : line + 1, lane : lane + LANES])
        return jnp.concatenate(lines, axis=1) if len(lines) > 1 else lines[0]

    def phase1(way, src, r1):
        out = []
        for o in range(1, group):
            p, dev = peer_of(o)
            c = pltpu.make_async_remote_copy(
                src_ref=src.at[p], dst_ref=r1.at[m], send_sem=s1.at[way, o],
                recv_sem=v1.at[way, m], device_id=dev, device_id_type=MESH)
            c.start()
            out.append(c)
        r1[pl.ds(m, 1)] = src[pl.ds(m, 1)]
        return out

    def wait1(way, src, r1):
        for o in range(1, group):
            p, dev = peer_of(o)
            pltpu.make_async_remote_copy(
                src_ref=src.at[p], dst_ref=r1.at[p], send_sem=s1.at[way, o],
                recv_sem=v1.at[way, p], device_id=dev, device_id_type=MESH).wait_recv()

    def phase2(way, r1, tot, r2):
        total = r1[0].astype(F32)
        for j in range(1, group):
            total = total + r1[j].astype(F32)
        total = total.astype(tot.dtype)
        tot[...] = total
        out = []
        for o in range(1, no):
            zp, dev = outer_of(o)
            c = pltpu.make_async_remote_copy(
                src_ref=tot, dst_ref=r2.at[z], send_sem=s2.at[way, o],
                recv_sem=v2.at[way, z], device_id=dev, device_id_type=MESH)
            c.start()
            out.append(c)
        r2[pl.ds(z, 1)] = total[None]
        return out

    def wait2(way, tot, r2):
        for o in range(1, no):
            zp, dev = outer_of(o)
            pltpu.make_async_remote_copy(
                src_ref=tot, dst_ref=r2.at[zp], send_sem=s2.at[way, o],
                recv_sem=v2.at[way, zp], device_id=dev, device_id_type=MESH).wait_recv()

    def phase3(way, r1, r2, res, r3):
        backward = way == 1
        run = jnp.zeros(tot_f.shape if way == 0 else tot_b.shape, F32)
        whole = run
        for zz in range(no):
            part = r2[zz].astype(F32)
            earlier = (zz > z) if backward else (zz < z)
            run = run + jnp.where(earlier, part, 0.0)
            whole = whole + part
        if backward:
            line = lax.broadcasted_iota(jnp.int32, run.shape, 0)
            tile = lax.broadcasted_iota(jnp.int32, run.shape, 1) // LANES
            extra = ((m - first) * per + tile) * 16 + line >= tiles
        for aa in (range(inner - 1, -1, -1) if backward else range(inner)):
            for bb in range(nb):
                run = run + r1[aa * nb + bb].astype(F32)
            res[aa] = (jnp.where(extra, whole, run) if backward else run).astype(res.dtype)
        out = []
        for o in range(1, group):
            p, dev = peer_of(o)
            c = pltpu.make_async_remote_copy(
                src_ref=res.at[peers[o][1]], dst_ref=r3.at[m], send_sem=s3.at[way, o],
                recv_sem=v3.at[way, m], device_id=dev, device_id_type=MESH)
            c.start()
            out.append(c)
        r3[pl.ds(m, 1)] = res[pl.ds(a, 1)]
        return out

    def wait3(way, res, r3):
        for o in range(1, group):
            p, dev = peer_of(o)
            pltpu.make_async_remote_copy(
                src_ref=res.at[peers[o][1]], dst_ref=r3.at[p], send_sem=s3.at[way, o],
                recv_sem=v3.at[way, p], device_id=dev, device_id_type=MESH).wait_recv()
        if way == 0:
            for tile in range(tiles):
                for h in range(4):
                    slot, lane = (4 * tile + h) // fper, (4 * tile + h) % fper * LANES
                    state[8 * h : 8 * h + 8, tile * LANES : (tile + 1) * LANES] = r3[
                        slot, :, lane : lane + LANES]
            return
        for tile in range(tiles):
            lane = (tile % per) * LANES
            for h in range(2):
                state[16 * h : 16 * h + 16, tile * LANES : (tile + 1) * LANES] = r3[
                    2 * (tile // per) + h, :, lane : lane + LANES].astype(F32)
        extra_s[...] = r3[first:group].astype(F32)

    def norm_of(at, size):
        lines = []
        for t in range(at // LANES, (at + size) // LANES):
            slot, line, lane = spot(t)
            lines.append(extra_s[slot - first, line : line + 1, lane : lane + LANES])
        return jnp.concatenate(lines, axis=1) if len(lines) > 1 else lines[0]

    outs = ((mixed_out, mixed_ref), (qg_out, qg_ref), (kg_out, kg_ref), (vg_out, vg_ref))

    def writes(n):
        held, ref = outs[n]
        return pltpu.make_async_copy(held, ref.at[0], out_sem.at[n])

    def write(n):
        writes(n).start()

    sent = []
    loaded(0)
    kf[:, 0:cols, 0:width] = feature(k_raw[...].astype(F32)).astype(BF16)
    loaded(1)
    vpad[1 : rows + 1, 0:cols, 0:width] = v_raw[...].astype(F32)
    for at, size in groups(wide):
        kg = kf[:, :, at : at + size].reshape(count, size)
        vg = vpad[1 : rows + 1, :, at : at + size].reshape(count, size).astype(BF16)
        own = compress(mm_at(kg, vg), masks[size])
        norm = jnp.sum(kg.astype(F32), axis=0, keepdims=True)
        put_forward(at, size, own, norm)
    pl.semaphore_wait(barrier, group - 1 + no - 1)
    sent += phase1(0, src_f, r1_f)

    @pl.when(band > 0)
    def _():
        for c in halo_copies(True):
            c.start()

    @pl.when(band < nb - 1)
    def _():
        for c in halo_copies(False):
            c.start()

    loaded(2)
    qf[:, 0:cols, 0:width] = feature(q_raw[...].astype(F32)).astype(BF16)
    loaded(3)
    gpad[1 : rows + 1, 0:cols, 0:width] = g_raw[...].astype(F32)
    loaded(4)
    for i in range(3):
        for j in range(3):
            wpad[3 * i + j : 3 * i + j + 1, 0:width] = w_raw[i, j : j + 1, :]

    def conv(t):
        lanes = pl.ds(pl.multiple_of(t * LANES, LANES), LANES)
        vb = vpad[:, :, lanes]
        gb = gpad[:, :, lanes]
        vs = (pltpu.roll(vb, 1, 1), vb, pltpu.roll(vb, COLS - 1, 1))
        gs = (pltpu.roll(gb, 1, 1), gb, pltpu.roll(gb, COLS - 1, 1))
        own = gb[1 : rows + 1]
        lo = jnp.zeros((rows, COLS, LANES), F32)
        vl = lo
        for i in range(3):
            for j in range(3):
                w = wpad[3 * i + j : 3 * i + j + 1, lanes].reshape(1, 1, LANES)
                near = vs[j][i : i + rows]
                lo = lo + w * near
                vl = vl + w * gs[2 - j][2 - i : 2 - i + rows]
                term = jnp.sum(jnp.sum(own * near, axis=0), axis=0, keepdims=True)
                kterm[3 * i + j : 3 * i + j + 1, lanes] = term
        loc[:, :, lanes] = lo
        vloc[:, :, lanes] = vl

    half = (tiles + 1) // 2
    wait1(0, src_f, r1_f)
    sent += phase2(0, r1_f, tot_f, r2_f)

    @pl.when(band > 0)
    def _():
        for c in halo_copies(False):
            c.wait_recv()

    @pl.when(band < nb - 1)
    def _():
        for c in halo_copies(True):
            c.wait_recv()

    for i, pad in enumerate((vpad, gpad)):
        pad[0, 0:cols, 0:width] = halo[i, 0].astype(F32)
        pad[rows + 1, 0:cols, 0:width] = halo[i, 1].astype(F32)
    pl.loop(0, half)(conv)
    wait2(0, tot_f, r2_f)
    sent += phase3(0, r1_f, r2_f, res_f, r3_f)
    pl.loop(half, tiles)(conv)
    for r in range(9):
        for t in range(tiles):
            slot, line, lane = spot(tiles * (r + 1) + t)
            stage[slot, line : line + 1, lane : lane + LANES] = kterm[
                r : r + 1, t * LANES : (t + 1) * LANES]
    wait3(0, res_f, r3_f)
    blocks = []
    for at, size in groups(wide):
        mask, one = masks[size], ones[size]
        high, low = expand(state[:, at : at + size], mask)
        norm = norm_forward(at, size)
        blocks.append((high, low, norm))
        qg = qf[:, :, at : at + size].reshape(count, size)
        gg = gpad[1 : rows + 1, :, at : at + size].reshape(count, size)
        dh, dl = parts_of(qg.astype(F32) * norm)
        den = mm(dh, one) + mm(dl, one)
        num = mm(qg, high) + mm(qg, low)
        rden = 1.0 / den
        attn = num * rden
        th, tl = parts_of(gg * attn)
        dgw = -(mm(th, one) + mm(tl, one)) * rden
        sh = (gg * rden).astype(BF16)
        own = compress(mm_at(qg, sh), mask)
        put(stage, at, size, own, jnp.sum(qg.astype(F32) * dgw, axis=0, keepdims=True))
        attn_s[:, at : at + size] = attn
        rden_s[:, at : at + size] = rden
        dgw_s[:, at : at + size] = dgw
    src_b[...] = stage[...].astype(BF16)
    sent += phase1(1, src_b, r1_b)
    mixed = (attn_s[...].reshape(rows, COLS, wide) + loc[...]).astype(BF16)
    mixed_out[...] = mixed[:, 0:cols, 0:width]
    write(0)
    wait1(1, src_b, r1_b)
    sent += phase2(1, r1_b, tot_b, r2_b)
    for (at, size), (high, low, norm) in zip(groups(wide), blocks):
        gg = gpad[1 : rows + 1, :, at : at + size].reshape(count, size)
        sh, sl = parts_of(gg * rden_s[:, at : at + size])
        back = mm_bt(sh, high) + mm_bt(sh, low) + mm_bt(sl, high)
        attn_s[:, at : at + size] = back + dgw_s[:, at : at + size] * norm
    grad = attn_s[...].reshape(rows, COLS, wide)[:, 0:cols, 0:width]
    qg_out[...] = (grad * slope(q_raw[...].astype(F32))).astype(BF16)
    write(1)
    wait2(1, tot_b, r2_b)
    sent += phase3(1, r1_b, r2_b, res_b, r3_b)
    for c in sent[: -(group - 1)]:
        c.wait_send()

    @pl.when(band > 0)
    def _():
        for c in halo_copies(True):
            c.wait_send()

    @pl.when(band < nb - 1)
    def _():
        for c in halo_copies(False):
            c.wait_send()

    steep = slope(k_raw[...].astype(F32))
    dgw_s[...] = jnp.ones_like(dgw_s)
    for r in range(rows):
        dgw_s[r * COLS : r * COLS + cols, 0:width] = steep[r]
    wait3(1, res_b, r3_b)

    def send_out(n, held, made):
        held[...] = made[...].reshape(rows, COLS, wide)[:, 0:cols, 0:width].astype(BF16)
        write(n)

    later = []
    for at, size in groups(wide):
        high = expand(state[:, at : at + size], masks[size])[0]
        norm = norm_of(at, size)
        later.append(high)
        vg = vpad[1 : rows + 1, :, at : at + size].reshape(count, size).astype(BF16)
        back = mm_bt(vg, high) + norm
        attn_s[:, at : at + size] = back * dgw_s[:, at : at + size]
    send_out(2, kg_out, attn_s)
    for (at, size), high in zip(groups(wide), later):
        kg = kf[:, :, at : at + size].reshape(count, size)
        rden_s[:, at : at + size] = mm(kg, high) + vloc[
            :, :, at : at + size].reshape(count, size)
    send_out(3, vg_out, rden_s)
    tokens = lax.axis_size("tm") * nb * rows * cols
    for r in range(9):
        for t in range(tiles):
            slot, line, lane = spot(tiles * (r + 1) + t)
            size = min(LANES, width - t * LANES)
            term = extra_s[slot - first, line : line + 1, lane : lane + size]
            wg_out[r // 3, r % 3 : r % 3 + 1, t * LANES : t * LANES + size] = term * (
                1.0 / math.sqrt(tokens))

    pltpu.make_async_copy(wg_out, wg_ref, out_sem.at[4]).start()
    for n in range(4):
        writes(n).wait()
    pltpu.make_async_copy(wg_out, wg_ref, out_sem.at[4]).wait()
    for c in sent[-(group - 1) :]:
        c.wait_send()


def shards(query_input, key_input, value_input, cotangent, local_kernel_weight):
    _, rows, cols, width = query_input.shape
    wide = -(-width // LANES) * LANES
    frames, nb = lax.axis_size("tm"), lax.axis_size("band")
    inner = 4
    no = frames // inner
    group = nb * inner
    tiles = wide // LANES
    per = -(-tiles // (group // 2))
    first = 2 * -(-tiles // per)
    lanes = per * LANES
    fper = -(-(4 * tiles + -(-tiles // 8)) // group)
    count = rows * COLS
    cfg = (rows, cols, width, wide, nb, no, inner, per, first, fper)
    raw = pltpu.VMEM((rows, cols, width), BF16)

    def buffers(r, lanes, kind):
        return [
            pltpu.VMEM((n, r, lanes) if n else (r, lanes), kind)
            for n in (group, group, 0, no, inner, group)
        ]

    tok = jax.ShapeDtypeStruct(query_input.shape, BF16)
    dma = pltpu.SemaphoreType.DMA
    made = pl.pallas_call(
        functools.partial(kernel, cfg),
        out_shape=(tok, tok, tok, tok, jax.ShapeDtypeStruct(local_kernel_weight.shape, F32)),
        in_specs=[pl.BlockSpec(memory_space=pltpu.HBM)] * 5,
        out_specs=[pl.BlockSpec(memory_space=pl.ANY)] * 5,
        scratch_shapes=[
            raw, raw, raw, raw, raw, raw, raw, raw,
            pltpu.VMEM(local_kernel_weight.shape, F32), dma((5,)),
            pltpu.VMEM((2, 2, cols, width), BF16),
            pltpu.VMEM((rows + 2, COLS, wide), F32), pltpu.VMEM((rows + 2, COLS, wide), F32),
            pltpu.VMEM((rows, COLS, wide), BF16), pltpu.VMEM((rows, COLS, wide), BF16),
            pltpu.VMEM((16, wide), F32),
            pltpu.VMEM((rows, COLS, wide), F32), pltpu.VMEM((rows, COLS, wide), F32),
            pltpu.VMEM((16, wide), F32),
            pltpu.VMEM((count, wide), F32), pltpu.VMEM((count, wide), F32),
            pltpu.VMEM((count, wide), F32),
            pltpu.VMEM((HEAD_DIM, wide), F32),
            pltpu.VMEM((group, 16, lanes), F32), pltpu.VMEM((group - first, 16, lanes), F32),
            pltpu.VMEM(local_kernel_weight.shape, F32),
            *buffers(8, fper * LANES, F32), *buffers(16, lanes, BF16),
            dma((5,)), dma((2, 2)), dma((2, 2)),
            dma((2, group)), dma((2, group)), dma((2, no)), dma((2, no)),
            dma((2, group)), dma((2, group)),
        ],
        compiler_params=pltpu.CompilerParams(
            collective_id=0, has_side_effects=True, vmem_limit_bytes=62 * 1024 * 1024
        ),
        cost_estimate=pl.CostEstimate(flops=10**9, bytes_accessed=3 * 10**6, transcendentals=0),
        name="block_causal",
    )(query_input, key_input, value_input, cotangent, local_kernel_weight)
    return pl.pallas_call(
        hand_over,
        out_shape=tuple(jax.ShapeDtypeStruct(x.shape, x.dtype) for x in made),
        in_specs=[pl.BlockSpec(memory_space=pl.ANY)] * 5,
        out_specs=[pl.BlockSpec(memory_space=pltpu.HBM)] * 5,
        scratch_shapes=[pltpu.VMEM(x.shape, x.dtype) for x in made]
        + [dma((5,)), dma((5,))],
        compiler_params=pltpu.CompilerParams(vmem_limit_bytes=62 * 1024 * 1024),
        name="hand_over",
    )(*made)


def hand_over(*refs):
    pieces = []
    for i in range(5):
        src, dst, held = refs[i], refs[5 + i], refs[10 + i]
        pieces.append((
            pltpu.make_async_copy(src, held, refs[15].at[i]),
            pltpu.make_async_copy(held, dst, refs[16].at[i]),
        ))
    for load, _ in pieces:
        load.start()
    for load, store in pieces:
        load.wait()
        store.start()
    for _, store in pieces:
        store.wait()


def solution(mesh):
    token = P("tm", "band", None, None)
    return jax.shard_map(
        shards,
        mesh=mesh,
        in_specs=(token,) * 4 + (P(),),
        out_specs=(token,) * 4 + (P(),),
        check_vma=False,
    )
```

```python
import functools
import math

import jax
import jax.numpy as jnp
from jax import lax
from jax.experimental import pallas as pl
from jax.experimental.pallas import tpu as pltpu
from jax.sharding import PartitionSpec as P

HEAD_DIM = 32
LANES = 128
COLS = 32
MESH = pl.DeviceIdType.MESH
F32 = jnp.float32
BF16 = jnp.bfloat16


def groups(wide):
    out, at = [], 0
    while at < wide:
        size = min(256, wide - at)
        out.append((at, size))
        at += size
    return out


def feature(x):
    return jnp.where(x > 0, x + 1.0, jnp.exp(jnp.minimum(x, 0.0)))


def slope(x):
    return jnp.where(x > 0, 1.0, jnp.exp(jnp.minimum(x, 0.0)))


def parts_of(x):
    high = x.astype(BF16)
    return high, (x - high.astype(F32)).astype(BF16)


def mm(a, b):
    return lax.dot_general(a, b, (((1,), (0,)), ((), ())), preferred_element_type=F32)


def mm_bt(a, b):
    return lax.dot_general(a, b, (((1,), (1,)), ((), ())), preferred_element_type=F32)


def mm_at(a, b):
    return lax.dot_general(a, b, (((0,), (0,)), ((), ())), preferred_element_type=F32)


def same_head(size):
    row = lax.broadcasted_iota(jnp.int32, (size, size), 0) // HEAD_DIM
    lane = lax.broadcasted_iota(jnp.int32, (size, size), 1) // HEAD_DIM
    return row == lane


def compress(full, mask):
    size = full.shape[0]
    kept = jnp.where(mask, full, 0.0)
    total = kept[0:HEAD_DIM]
    for h in range(1, size // HEAD_DIM):
        total = total + kept[h * HEAD_DIM : (h + 1) * HEAD_DIM]
    return total


def expand(compact, mask):
    size = compact.shape[1]
    tiled = jnp.concatenate([compact] * (size // HEAD_DIM), axis=0)
    return parts_of(jnp.where(mask, tiled, 0.0))


def kernel(cfg, q_hbm, k_hbm, v_hbm, g_hbm, w_hbm, mixed_ref, qg_ref, kg_ref, vg_ref, wg_ref,
           q_raw, k_raw, v_raw, g_raw, mixed_out, qg_out, kg_out, vg_out, wg_out, out_sem, halo, vpad, gpad, qf, kf, wpad, loc, vloc, kterm,
           attn_s, rden_s, dgw_s, state, stage, extra_s, w_raw, src_f, r1_f, tot_f, r2_f, res_f, r3_f,
           src_b, r1_b, tot_b, r2_b, res_b, r3_b,
           in_sem, halo_send, halo_recv, s1, v1, s2, v2, s3, v3):
    rows, cols, width, wide, nb, no, inner, per, first, fper = cfg
    group = nb * inner
    count = rows * COLS
    tm = lax.axis_index("tm")
    band = lax.axis_index("band")
    z = tm // inner
    tiles = wide // LANES
    a = tm % inner
    m = a * nb + band

    def placed(p):
        frame = lax.div(p, nb)
        return p, frame, {"tm": z * inner + frame, "band": lax.rem(p, nb)}

    peers = [None] + [placed(lax.rem(m + o, group)) for o in range(1, group)]
    outers = [lax.rem(z + o, no) for o in range(no)]

    def peer_of(o):
        return peers[o][0], peers[o][2]

    def outer_of(o):
        return outers[o], {"tm": outers[o] * inner + a, "band": band}

    loads = [
        pltpu.make_async_copy(h.at[0], d, in_sem.at[i])
        for i, (h, d) in enumerate(((k_hbm, k_raw), (v_hbm, v_raw), (q_hbm, q_raw), (g_hbm, g_raw)))
    ]
    loads.append(pltpu.make_async_copy(w_hbm, w_raw, in_sem.at[4]))
    for c in loads[:2]:
        c.start()

    def loaded(i):
        loads[i].wait()

    halo[...] = jnp.zeros_like(halo)
    barrier = pltpu.get_barrier_semaphore()
    for o in range(1, group):
        pl.semaphore_signal(barrier, inc=1, device_id=peer_of(o)[1], device_id_type=MESH)
    for o in range(1, no):
        pl.semaphore_signal(barrier, inc=1, device_id=outer_of(o)[1], device_id_type=MESH)

    for c in loads[2:]:
        c.start()
    vpad[...] = jnp.zeros_like(vpad)
    gpad[...] = jnp.zeros_like(gpad)
    kf[...] = jnp.zeros_like(kf)
    kf[:, 0:cols, width:wide] = jnp.ones((rows, cols, wide - width), BF16)
    qf[...] = jnp.ones_like(qf)
    wpad[...] = jnp.zeros_like(wpad)
    src_f[...] = jnp.zeros_like(src_f)
    stage[...] = jnp.zeros_like(stage)

    def halo_copies(up):
        out = []
        for i, h in enumerate((v_hbm, g_hbm)):
            out.append(pltpu.make_async_remote_copy(
                src_ref=h.at[0, 0] if up else h.at[0, rows - 1],
                dst_ref=halo.at[i, 1 if up else 0],
                send_sem=halo_send.at[i, 1 if up else 0],
                recv_sem=halo_recv.at[i, 1 if up else 0],
                device_id={"band": band - 1 if up else band + 1},
                device_id_type=MESH,
            ))
        return out

    masks = {size: same_head(size) for _, size in groups(wide)}
    ones = {size: masks[size].astype(F32).astype(BF16) for size in masks}

    def spot(index):
        line = index % 16
        tile = index // 16
        return first + tile // per, line, (tile % per) * LANES

    def put(dst, at, size, compact, norm):
        for t in range(size // LANES):
            tile = at // LANES + t
            lane = (tile % per) * LANES
            for h in range(2):
                dst[2 * (tile // per) + h, :, lane : lane + LANES] = compact[
                    16 * h : 16 * h + 16, t * LANES : (t + 1) * LANES]
            slot, line, lane = spot(tile)
            dst[slot, line : line + 1, lane : lane + LANES] = norm[
                :, t * LANES : (t + 1) * LANES]

    def put_forward(at, size, compact, norm):
        for t in range(size // LANES):
            tile = at // LANES + t
            part = slice(t * LANES, (t + 1) * LANES)
            for h in range(4):
                slot, lane = (4 * tile + h) // fper, (4 * tile + h) % fper * LANES
                src_f[slot, :, lane : lane + LANES] = compact[8 * h : 8 * h + 8, part]
            piece = 4 * tiles + tile // 8
            slot, lane, line = piece // fper, piece % fper * LANES, tile % 8
            src_f[slot, line : line + 1, lane : lane + LANES] = norm[:, part]

    def norm_forward(at, size):
        lines = []
        for tile in range(at // LANES, (at + size) // LANES):
            piece = 4 * tiles + tile // 8
            slot, lane, line = piece // fper, piece % fper * LANES, tile % 8
            lines.append(r3_f[slot, line : line + 1, lane : lane + LANES])
        return jnp.concatenate(lines, axis=1) if len(lines) > 1 else lines[0]

    def phase1(way, src, r1):
        out = []
        for o in sorted(range(1, group), key=lambda n: -min(n, group - n)):
            p, dev = peer_of(o)
            c = pltpu.make_async_remote_copy(
                src_ref=src.at[p], dst_ref=r1.at[m], send_sem=s1.at[way, o],
                recv_sem=v1.at[way, m], device_id=dev, device_id_type=MESH)
            c.start()
            out.append(c)
        r1[pl.ds(m, 1)] = src[pl.ds(m, 1)]
        return out

    def wait1(way, src, r1):
        for o in range(1, group):
            p, dev = peer_of(o)
            pltpu.make_async_remote_copy(
                src_ref=src.at[p], dst_ref=r1.at[p], send_sem=s1.at[way, o],
                recv_sem=v1.at[way, p], device_id=dev, device_id_type=MESH).wait_recv()

    def phase2(way, r1, tot, r2):
        total = r1[0].astype(F32)
        for j in range(1, group):
            total = total + r1[j].astype(F32)
        total = total.astype(tot.dtype)
        tot[...] = total
        out = []
        for o in range(1, no):
            zp, dev = outer_of(o)
            c = pltpu.make_async_remote_copy(
                src_ref=tot, dst_ref=r2.at[z], send_sem=s2.at[way, o],
                recv_sem=v2.at[way, z], device_id=dev, device_id_type=MESH)
            c.start()
            out.append(c)
        r2[pl.ds(z, 1)] = total[None]
        return out

    def wait2(way, tot, r2):
        for o in range(1, no):
            zp, dev = outer_of(o)
            pltpu.make_async_remote_copy(
                src_ref=tot, dst_ref=r2.at[zp], send_sem=s2.at[way, o],
                recv_sem=v2.at[way, zp], device_id=dev, device_id_type=MESH).wait_recv()

    def phase3(way, r1, r2, res, r3):
        backward = way == 1
        run = jnp.zeros(tot_f.shape if way == 0 else tot_b.shape, F32)
        whole = run
        for zz in range(no):
            part = r2[zz].astype(F32)
            earlier = (zz > z) if backward else (zz < z)
            run = run + jnp.where(earlier, part, 0.0)
            whole = whole + part
        if backward:
            line = lax.broadcasted_iota(jnp.int32, run.shape, 0)
            tile = lax.broadcasted_iota(jnp.int32, run.shape, 1) // LANES
            extra = ((m - first) * per + tile) * 16 + line >= tiles
        for aa in (range(inner - 1, -1, -1) if backward else range(inner)):
            for bb in range(nb):
                run = run + r1[aa * nb + bb].astype(F32)
            res[aa] = (jnp.where(extra, whole, run) if backward else run).astype(res.dtype)
        out = []
        for o in sorted(range(1, group), key=lambda n: -min(n, group - n)):
            p, dev = peer_of(o)
            c = pltpu.make_async_remote_copy(
                src_ref=res.at[peers[o][1]], dst_ref=r3.at[m], send_sem=s3.at[way, o],
                recv_sem=v3.at[way, m], device_id=dev, device_id_type=MESH)
            c.start()
            out.append(c)
        r3[pl.ds(m, 1)] = res[pl.ds(a, 1)]
        return out

    def wait3(way, res, r3):
        for o in range(1, group):
            p, dev = peer_of(o)
            pltpu.make_async_remote_copy(
                src_ref=res.at[peers[o][1]], dst_ref=r3.at[p], send_sem=s3.at[way, o],
                recv_sem=v3.at[way, p], device_id=dev, device_id_type=MESH).wait_recv()
        if way == 0:
            for tile in range(tiles):
                for h in range(4):
                    slot, lane = (4 * tile + h) // fper, (4 * tile + h) % fper * LANES
                    state[8 * h : 8 * h + 8, tile * LANES : (tile + 1) * LANES] = r3[
                        slot, :, lane : lane + LANES]
            return
        for tile in range(tiles):
            lane = (tile % per) * LANES
            for h in range(2):
                state[16 * h : 16 * h + 16, tile * LANES : (tile + 1) * LANES] = r3[
                    2 * (tile // per) + h, :, lane : lane + LANES].astype(F32)
        extra_s[...] = r3[first:group].astype(F32)

    def norm_of(at, size):
        lines = []
        for t in range(at // LANES, (at + size) // LANES):
            slot, line, lane = spot(t)
            lines.append(extra_s[slot - first, line : line + 1, lane : lane + LANES])
        return jnp.concatenate(lines, axis=1) if len(lines) > 1 else lines[0]

    outs = ((mixed_out, mixed_ref), (qg_out, qg_ref), (kg_out, kg_ref), (vg_out, vg_ref))

    def writes(n):
        held, ref = outs[n]
        return pltpu.make_async_copy(held, ref.at[0], out_sem.at[n])

    def write(n):
        writes(n).start()

    sent = []
    loaded(0)
    kf[:, 0:cols, 0:width] = feature(k_raw[...].astype(F32)).astype(BF16)
    loaded(1)
    vpad[1 : rows + 1, 0:cols, 0:width] = v_raw[...].astype(F32)
    for at, size in groups(wide):
        kg = kf[:, :, at : at + size].reshape(count, size)
        vg = vpad[1 : rows + 1, :, at : at + size].reshape(count, size).astype(BF16)
        own = compress(mm_at(kg, vg), masks[size])
        norm = jnp.sum(kg.astype(F32), axis=0, keepdims=True)
        put_forward(at, size, own, norm)
    pl.semaphore_wait(barrier, group - 1 + no - 1)
    sent += phase1(0, src_f, r1_f)

    @pl.when(band > 0)
    def _():
        for c in halo_copies(True):
            c.start()

    @pl.when(band < nb - 1)
    def _():
        for c in halo_copies(False):
            c.start()

    loaded(2)
    qf[:, 0:cols, 0:width] = feature(q_raw[...].astype(F32)).astype(BF16)
    loaded(3)
    gpad[1 : rows + 1, 0:cols, 0:width] = g_raw[...].astype(F32)
    loaded(4)
    for i in range(3):
        for j in range(3):
            wpad[3 * i + j : 3 * i + j + 1, 0:width] = w_raw[i, j : j + 1, :]

    def conv(t):
        lanes = pl.ds(pl.multiple_of(t * LANES, LANES), LANES)
        vb = vpad[:, :, lanes]
        gb = gpad[:, :, lanes]
        vs = (pltpu.roll(vb, 1, 1), vb, pltpu.roll(vb, COLS - 1, 1))
        gs = (pltpu.roll(gb, 1, 1), gb, pltpu.roll(gb, COLS - 1, 1))
        own = gb[1 : rows + 1]
        lo = jnp.zeros((rows, COLS, LANES), F32)
        vl = lo
        for i in range(3):
            for j in range(3):
                w = wpad[3 * i + j : 3 * i + j + 1, lanes].reshape(1, 1, LANES)
                near = vs[j][i : i + rows]
                lo = lo + w * near
                vl = vl + w * gs[2 - j][2 - i : 2 - i + rows]
                term = jnp.sum(jnp.sum(own * near, axis=0), axis=0, keepdims=True)
                kterm[3 * i + j : 3 * i + j + 1, lanes] = term
        loc[:, :, lanes] = lo
        vloc[:, :, lanes] = vl

    half = (tiles + 1) // 2
    wait1(0, src_f, r1_f)
    sent += phase2(0, r1_f, tot_f, r2_f)

    @pl.when(band > 0)
    def _():
        for c in halo_copies(False):
            c.wait_recv()

    @pl.when(band < nb - 1)
    def _():
        for c in halo_copies(True):
            c.wait_recv()

    for i, pad in enumerate((vpad, gpad)):
        pad[0, 0:cols, 0:width] = halo[i, 0].astype(F32)
        pad[rows + 1, 0:cols, 0:width] = halo[i, 1].astype(F32)
    pl.loop(0, half)(conv)
    wait2(0, tot_f, r2_f)
    sent += phase3(0, r1_f, r2_f, res_f, r3_f)
    pl.loop(half, tiles)(conv)
    for r in range(9):
        for t in range(tiles):
            slot, line, lane = spot(tiles * (r + 1) + t)
            stage[slot, line : line + 1, lane : lane + LANES] = kterm[
                r : r + 1, t * LANES : (t + 1) * LANES]
    wait3(0, res_f, r3_f)
    blocks = []
    for at, size in groups(wide):
        mask, one = masks[size], ones[size]
        high, low = expand(state[:, at : at + size], mask)
        norm = norm_forward(at, size)
        blocks.append((high, low, norm))
        qg = qf[:, :, at : at + size].reshape(count, size)
        gg = gpad[1 : rows + 1, :, at : at + size].reshape(count, size)
        dh, dl = parts_of(qg.astype(F32) * norm)
        den = mm(dh, one) + mm(dl, one)
        num = mm(qg, high) + mm(qg, low)
        rden = 1.0 / den
        attn = num * rden
        th, tl = parts_of(gg * attn)
        dgw = -(mm(th, one) + mm(tl, one)) * rden
        sh = (gg * rden).astype(BF16)
        own = compress(mm_at(qg, sh), mask)
        put(stage, at, size, own, jnp.sum(qg.astype(F32) * dgw, axis=0, keepdims=True))
        attn_s[:, at : at + size] = attn
        rden_s[:, at : at + size] = rden
        dgw_s[:, at : at + size] = dgw
    src_b[...] = stage[...].astype(BF16)
    sent += phase1(1, src_b, r1_b)
    mixed = (attn_s[...].reshape(rows, COLS, wide) + loc[...]).astype(BF16)
    mixed_out[...] = mixed[:, 0:cols, 0:width]
    write(0)
    wait1(1, src_b, r1_b)
    sent += phase2(1, r1_b, tot_b, r2_b)
    for (at, size), (high, low, norm) in zip(groups(wide), blocks):
        gg = gpad[1 : rows + 1, :, at : at + size].reshape(count, size)
        sh, sl = parts_of(gg * rden_s[:, at : at + size])
        back = mm_bt(sh, high) + mm_bt(sh, low) + mm_bt(sl, high)
        attn_s[:, at : at + size] = back + dgw_s[:, at : at + size] * norm
    grad = attn_s[...].reshape(rows, COLS, wide)[:, 0:cols, 0:width]
    qg_out[...] = (grad * slope(q_raw[...].astype(F32))).astype(BF16)
    write(1)
    wait2(1, tot_b, r2_b)
    sent += phase3(1, r1_b, r2_b, res_b, r3_b)
    for c in sent[: -(group - 1)]:
        c.wait_send()

    @pl.when(band > 0)
    def _():
        for c in halo_copies(True):
            c.wait_send()

    @pl.when(band < nb - 1)
    def _():
        for c in halo_copies(False):
            c.wait_send()

    steep = slope(k_raw[...].astype(F32))
    dgw_s[...] = jnp.ones_like(dgw_s)
    for r in range(rows):
        dgw_s[r * COLS : r * COLS + cols, 0:width] = steep[r]
    wait3(1, res_b, r3_b)

    def send_out(n, held, made):
        held[...] = made[...].reshape(rows, COLS, wide)[:, 0:cols, 0:width].astype(BF16)
        write(n)

    later = []
    for at, size in groups(wide):
        high = expand(state[:, at : at + size], masks[size])[0]
        norm = norm_of(at, size)
        later.append(high)
        vg = vpad[1 : rows + 1, :, at : at + size].reshape(count, size).astype(BF16)
        back = mm_bt(vg, high) + norm
        attn_s[:, at : at + size] = back * dgw_s[:, at : at + size]
    send_out(2, kg_out, attn_s)
    for (at, size), high in zip(groups(wide), later):
        kg = kf[:, :, at : at + size].reshape(count, size)
        rden_s[:, at : at + size] = mm(kg, high) + vloc[
            :, :, at : at + size].reshape(count, size)
    send_out(3, vg_out, rden_s)
    tokens = lax.axis_size("tm") * nb * rows * cols
    for r in range(9):
        for t in range(tiles):
            slot, line, lane = spot(tiles * (r + 1) + t)
            size = min(LANES, width - t * LANES)
            term = extra_s[slot - first, line : line + 1, lane : lane + size]
            wg_out[r // 3, r % 3 : r % 3 + 1, t * LANES : t * LANES + size] = term * (
                1.0 / math.sqrt(tokens))

    pltpu.make_async_copy(wg_out, wg_ref, out_sem.at[4]).start()
    for n in range(4):
        writes(n).wait()
    pltpu.make_async_copy(wg_out, wg_ref, out_sem.at[4]).wait()
    for c in sent[-(group - 1) :]:
        c.wait_send()


def shards(query_input, key_input, value_input, cotangent, local_kernel_weight):
    _, rows, cols, width = query_input.shape
    wide = -(-width // LANES) * LANES
    frames, nb = lax.axis_size("tm"), lax.axis_size("band")
    inner = 4
    no = frames // inner
    group = nb * inner
    tiles = wide // LANES
    per = -(-tiles // (group // 2))
    first = 2 * -(-tiles // per)
    lanes = per * LANES
    fper = -(-(4 * tiles + -(-tiles // 8)) // group)
    count = rows * COLS
    cfg = (rows, cols, width, wide, nb, no, inner, per, first, fper)
    raw = pltpu.VMEM((rows, cols, width), BF16)

    def buffers(r, lanes, kind):
        return [
            pltpu.VMEM((n, r, lanes) if n else (r, lanes), kind)
            for n in (group, group, 0, no, inner, group)
        ]

    tok = jax.ShapeDtypeStruct(query_input.shape, BF16)
    dma = pltpu.SemaphoreType.DMA
    made = pl.pallas_call(
        functools.partial(kernel, cfg),
        out_shape=(tok, tok, tok, tok, jax.ShapeDtypeStruct(local_kernel_weight.shape, F32)),
        in_specs=[pl.BlockSpec(memory_space=pltpu.HBM)] * 5,
        out_specs=[pl.BlockSpec(memory_space=pl.ANY)] * 5,
        scratch_shapes=[
            raw, raw, raw, raw, raw, raw, raw, raw,
            pltpu.VMEM(local_kernel_weight.shape, F32), dma((5,)),
            pltpu.VMEM((2, 2, cols, width), BF16),
            pltpu.VMEM((rows + 2, COLS, wide), F32), pltpu.VMEM((rows + 2, COLS, wide), F32),
            pltpu.VMEM((rows, COLS, wide), BF16), pltpu.VMEM((rows, COLS, wide), BF16),
            pltpu.VMEM((16, wide), F32),
            pltpu.VMEM((rows, COLS, wide), F32), pltpu.VMEM((rows, COLS, wide), F32),
            pltpu.VMEM((16, wide), F32),
            pltpu.VMEM((count, wide), F32), pltpu.VMEM((count, wide), F32),
            pltpu.VMEM((count, wide), F32),
            pltpu.VMEM((HEAD_DIM, wide), F32),
            pltpu.VMEM((group, 16, lanes), F32), pltpu.VMEM((group - first, 16, lanes), F32),
            pltpu.VMEM(local_kernel_weight.shape, F32),
            *buffers(8, fper * LANES, F32), *buffers(16, lanes, BF16),
            dma((5,)), dma((2, 2)), dma((2, 2)),
            dma((2, group)), dma((2, group)), dma((2, no)), dma((2, no)),
            dma((2, group)), dma((2, group)),
        ],
        compiler_params=pltpu.CompilerParams(
            collective_id=0, has_side_effects=True, vmem_limit_bytes=62 * 1024 * 1024
        ),
        cost_estimate=pl.CostEstimate(flops=10**9, bytes_accessed=3 * 10**6, transcendentals=0),
        name="block_causal",
    )(query_input, key_input, value_input, cotangent, local_kernel_weight)
    return pl.pallas_call(
        hand_over,
        out_shape=tuple(jax.ShapeDtypeStruct(x.shape, x.dtype) for x in made),
        in_specs=[pl.BlockSpec(memory_space=pl.ANY)] * 5,
        out_specs=[pl.BlockSpec(memory_space=pltpu.HBM)] * 5,
        scratch_shapes=[pltpu.VMEM(x.shape, x.dtype) for x in made]
        + [dma((5,)), dma((5,))],
        compiler_params=pltpu.CompilerParams(vmem_limit_bytes=62 * 1024 * 1024),
        name="hand_over",
    )(*made)


def hand_over(*refs):
    pieces = []
    for i in range(5):
        src, dst, held = refs[i], refs[5 + i], refs[10 + i]
        pieces.append((
            pltpu.make_async_copy(src, held, refs[15].at[i]),
            pltpu.make_async_copy(held, dst, refs[16].at[i]),
        ))
    for load, _ in pieces:
        load.start()
    for load, store in pieces:
        load.wait()
        store.start()
    for _, store in pieces:
        store.wait()


def solution(mesh):
    token = P("tm", "band", None, None)
    return jax.shard_map(
        shards,
        mesh=mesh,
        in_specs=(token,) * 4 + (P(),),
        out_specs=(token,) * 4 + (P(),),
        check_vma=False,
    )
```
